32 devices in a mesh: blk: 16 (over z, y, core), fld: 2 (over x).
Axes of the slice: x: 2, y: 2, z: 4, core: 2. Of those that a mesh axis runs over, the one named last changes fastest.
Arguments:
- vectors: bfloat16 [1024, 16384], P('blk', 'fld'), may hold values from -1.1953125 to 1.1953125
- norms: bfloat16 [1024], P('blk'), may hold values from 0.5 to 2
- offsets: int32 [2], replicated, may hold values from 1 to 7
- pivot_block: int32 [2, 3], replicated, may hold values from 0 to 15
- pivot_row: int32 [2, 3], replicated, may hold values from 0 to 63
Outputs:
- similarity: bfloat16 [2, 3, 1024, 64], P(None, None, ('blk', 'fld'))
The draws below stay inside these ranges and needn't reach their ends.
All inputs are finite; a program needn't handle non-finite values.
Results may differ from the reference program's by a relative error of at most 0.014.
Values may be sent and summed in bfloat16 or wider, within the bound.
A program may use at most 64 MiB of HBM per device.

```python
import math
import jax
import jax.numpy as jnp
from jax import lax

F = 16384
VB = 64
PIV = 3
NOFF = 2
NV = 1024
N_BLK = 16
N_FLD = 2


def place_ends(entries, rng, least, high):
    shape = entries.shape
    spot = [jax.random.randint(jax.random.fold_in(rng, axis), (), 0, shape[axis]) for axis in range(len(shape))]
    entries = entries.at[tuple(spot)].set(least)
    longest = shape.index(max(shape))
    spot[longest] = (spot[longest] + 1) % shape[longest]
    return entries.at[tuple(spot)].set(high)


def block_scale(own_key, extent, cuts, low, high):
    loudness, own = 1.0, jax.random.fold_in(own_key, 6)
    for dim, parts in cuts:
        draws = jnp.exp(jax.random.uniform(jax.random.fold_in(own, dim), (parts,), jnp.float32, low / len(cuts), high / len(cuts)))
        loudness = loudness * jnp.repeat(draws, extent[dim] // parts).reshape([-1 if axis == dim else 1 for axis in range(len(extent))])
    return loudness


def gaussian(own_key, dims, deviation, reach, shards=(), held_as=jnp.bfloat16):
    entries = jax.random.normal(own_key, dims, jnp.float32) * deviation
    if len(shards) > 0:
        entries = block_scale(own_key, dims, shards, -0.22, 0.18) * entries
    return jnp.clip(entries, min=-reach, max=reach).astype(held_as)


def setup_inputs(seed: int = 0) -> dict:
    key_of = jax.random.split(jax.random.key(seed), 6)
    vectors = gaussian(key_of[0], (NV, F), 0.2, 1.1953125, ((0, 16), (1, 2)))
    norms = jnp.clip(jnp.exp(math.log(2.0) - 1.3862944 * jax.random.uniform(key_of[1], (NV,), jnp.float32) ** block_scale(key_of[1], (NV,), ((0, 16),), -0.2, 0.2)), 0.5, 2.0).astype(jnp.bfloat16)
    offsets = jax.random.randint(key_of[2], (NOFF,), 1, N_BLK // 2).astype(jnp.int32)
    pivot_block = place_ends(jax.random.randint(key_of[3], (NOFF, PIV), 0, N_BLK), jax.random.fold_in(key_of[3], 1), 0, N_BLK - 1).astype(jnp.int32)
    pivot_row = place_ends(jax.random.randint(key_of[4], (NOFF, PIV), 0, VB), jax.random.fold_in(key_of[4], 1), 0, VB - 1).astype(jnp.int32)
    return dict(vectors=vectors, norms=norms, offsets=offsets, pivot_block=pivot_block, pivot_row=pivot_row)


def reference(vectors, norms, offsets, pivot_block, pivot_row):
    fd = F // N_FLD
    flat_index = (pivot_block * VB + pivot_row).reshape(-1).astype(jnp.int32)
    pivots = vectors[flat_index].astype(jnp.float32).reshape(NOFF, PIV, F)
    pivot_norms = norms[flat_index].astype(jnp.float32).reshape(NOFF, PIV)

    def one_block(block):
        start = (block * VB).astype(jnp.int32)
        resident = lax.dynamic_slice_in_dim(vectors, start, VB, 0)
        resident_norms = lax.dynamic_slice_in_dim(norms, start, VB, 0).astype(jnp.float32)

        def partner_of(offset):
            first = (((block + offset) % N_BLK) * VB).astype(jnp.int32)
            return (lax.dynamic_slice_in_dim(vectors, first, VB, 0),
                    lax.dynamic_slice_in_dim(norms, first, VB, 0))

        partners, partner_norms = jax.vmap(partner_of)(offsets)
        scaled = (resident.astype(jnp.float32)[None, None] * pivots[:, :, None, :]).astype(jnp.bfloat16)
        scaled = scaled.astype(jnp.float32).reshape(NOFF, PIV, VB, N_FLD, fd)
        partner_f = partners.astype(jnp.float32).reshape(NOFF, VB, N_FLD, fd)
        sums = jnp.einsum("tsinq,tknq->tsnik", scaled, partner_f, precision=lax.Precision.HIGHEST)
        rounded = lax.optimization_barrier(sums.astype(jnp.bfloat16))
        field_sum = jnp.sum(rounded.astype(jnp.float32), axis=2)
        denominator = (resident_norms[None, None, :, None] * pivot_norms[:, :, None, None]) * partner_norms.astype(jnp.float32)[:, None, None, :]
        return (field_sum / denominator).astype(jnp.bfloat16)

    tiles = lax.map(one_block, jnp.arange(N_BLK, dtype=jnp.int32))
    return jnp.transpose(tiles, (1, 2, 0, 3, 4)).reshape(NOFF, PIV, NV, VB)
```

```python
import functools

import jax
import jax.numpy as jnp
from jax import lax
from jax.experimental import pallas as pl
from jax.experimental.pallas import tpu as pltpu
from jax.sharding import PartitionSpec as P

MESH = pl.DeviceIdType.MESH
LANES = 128


def kernel(
    dims, offsets, pivot_block, pivot_row, vectors, norms, out,
    gat, norm_src, norm_all, piv, acc, part, mate_in, total, recv,
    send1, recv1, own1, sendn, recvn, send2, recv2, send3, recv3,
):
    N, NF, G, C, subs, groups, rows, noff, npiv = dims
    share = rows // NF
    halves = NF // 2
    width = C // subs
    per = G // groups
    me, place = lax.axis_index("blk"), lax.axis_index("fld")
    group, chunk = me // G, me % G
    base = group * G
    core = me % 2
    mate = me + 1 - 2 * core
    slot = (chunk // 2) * NF + place

    barrier = pltpu.get_barrier_semaphore()

    def greet_blk(j, carry):
        pl.semaphore_signal(
            barrier, inc=1, device_id=(lax.rem(me + j, N), place), device_id_type=MESH
        )
        return carry

    def greet_fld(j, carry):
        other = lax.rem(place + 1 + j // G, NF)
        pl.semaphore_signal(
            barrier, inc=1, device_id=(base + j % G, other), device_id_type=MESH
        )
        return carry

    lax.fori_loop(1, N, greet_blk, 0)
    lax.fori_loop(0, G * (NF - 1), greet_fld, 0)

    norm_src[...] = jnp.zeros_like(norm_src)
    norm_src[0:1, 0:rows] = norms[...].astype(jnp.float32)
    norm_all[me] = norm_src[...]
    for sub in range(subs):
        pltpu.make_async_copy(
            vectors.at[:, pl.ds(pl.multiple_of(chunk * C + sub * width, LANES), width)],
            gat[sub].at[me], own1.at[sub],
        ).start()
    pl.semaphore_wait(barrier, (N - 1) + G * (NF - 1))

    def shift(k):
        d = (k + 1) // 2
        return N // 2 + d * (2 * (k % 2) - 1)

    def block_copy(sub, k):
        j = shift(k)
        peer = lax.rem(me + j, N)
        first = pl.multiple_of((peer % G) * C + sub * width, LANES)
        return pltpu.make_async_remote_copy(
            src_ref=vectors.at[:, pl.ds(first, width)], dst_ref=gat[sub].at[me],
            send_sem=send1.at[sub, j], recv_sem=recv1.at[sub, j],
            device_id=(peer, place), device_id_type=MESH,
        )

    def norm_copy(k):
        j = shift(k)
        peer = lax.rem(me + j, N)
        return pltpu.make_async_remote_copy(
            src_ref=norm_src, dst_ref=norm_all.at[me],
            send_sem=sendn.at[j], recv_sem=recvn.at[j],
            device_id=(peer, place), device_id_type=MESH,
        )

    def loop(count, step):
        def run(k, carry):
            step(k)
            return carry

        lax.fori_loop(0, count, run, 0)

    for sub in range(subs):
        loop(N - 1, lambda k, sub=sub: block_copy(sub, k).start())
    loop(N - 1, lambda k: norm_copy(k).start())

    def pivots(sub):
        spot = lax.broadcasted_iota(jnp.int32, (rows, width), 0)
        for t in range(noff):
            for s in range(npiv):
                block = gat[sub][pivot_block[t, s]].astype(jnp.float32)
                picked = jnp.sum(
                    jnp.where(spot == pivot_row[t, s], block, 0.0), axis=0, keepdims=True
                )
                piv[t * npiv + s] = jnp.broadcast_to(picked, (16, width)).astype(jnp.bfloat16)

    def tile(sub, i):
        block = base + i
        resident = gat[sub][block].reshape(rows // 16, 16, width)
        found = []
        for t in range(noff):
            partner = gat[sub][lax.rem(block + offsets[t], N)]
            scaled = jnp.concatenate(
                [
                    (resident * piv[t * npiv + s][None]).reshape(rows, width)
                    for s in range(npiv)
                ],
                axis=0,
            )
            found.append(
                lax.dot_general(
                    scaled, partner, (((1,), (1,)), ((), ())),
                    preferred_element_type=jnp.float32,
                )
            )
        value = jnp.concatenate(found, axis=1)
        for s in range(npiv):
            for h in range(NF):
                first = s * rows + h * share
                piece = value[first : first + share]
                if sub > 0:
                    piece = piece + acc[i, h % 2, h // 2, s]
                acc[i, h % 2, h // 2, s] = piece

    def mate_copy(q):
        return pltpu.make_async_remote_copy(
            src_ref=part.at[q], dst_ref=mate_in.at[q],
            send_sem=send2.at[q], recv_sem=recv2.at[q],
            device_id=(mate, place), device_id_type=MESH,
        )

    def total_copy(i, q):
        return pltpu.make_async_remote_copy(
            src_ref=total.at[i, q], dst_ref=recv.at[slot],
            send_sem=send3.at[i, q], recv_sem=recv3.at[slot],
            device_id=(base + i, 2 * q + core), device_id_type=MESH,
        )

    def is_self(i, q):
        return jnp.logical_and(base + i == me, 2 * q + core == place)

    def hand_out(g):
        mate_copy(g).wait_recv()

        def one(k):
            i = g * per + k
            total[i] = (acc[i, core] + mate_in[g, k].astype(jnp.float32)).astype(total.dtype)
            for q in range(halves):
                here = is_self(i, q)

                @pl.when(here)
                def _():
                    pltpu.make_async_copy(total.at[i, q], recv.at[slot], recv3.at[slot]).start()

                @pl.when(jnp.logical_not(here))
                def _():
                    total_copy(i, q).start()

        loop(per, one)

    for sub in range(subs):
        pltpu.make_async_copy(
            vectors.at[:, pl.ds(pl.multiple_of(chunk * C + sub * width, LANES), width)],
            gat[sub].at[me], own1.at[sub],
        ).wait()
        loop(N - 1, lambda k, sub=sub: block_copy(sub, k).wait_recv())
        pivots(sub)
        if sub < subs - 1:
            loop(G, lambda i, sub=sub: tile(sub, i))
    for g in range(groups):
        def one(k, g=g):
            i = g * per + k
            tile(subs - 1, i)
            part[g, k] = acc[i, 1 - core].astype(part.dtype)

        loop(per, one)
        mate_copy(g).start()
        if g > 0:
            hand_out(g - 1)
    hand_out(groups - 1)

    loop(N - 1, lambda k: norm_copy(k).wait_recv())
    lane = lax.broadcasted_iota(jnp.int32, (1, LANES), 1)
    line = lax.broadcasted_iota(jnp.int32, (share, LANES), 0)
    cols = lax.broadcasted_iota(jnp.int32, (share, LANES), 1)
    own_norms = jnp.sum(
        jnp.where(cols == line + place * share, norm_src[0:1, :], 0.0), axis=1, keepdims=True
    )
    partner_norms = [norm_all[lax.rem(me + offsets[t], N)][0:1, 0:rows] for t in range(noff)]
    divisors = []
    for t in range(noff):
        for s in range(npiv):
            row = norm_all[pivot_block[t, s]][0:1, :]
            pivot_norm = jnp.sum(
                jnp.where(lane == pivot_row[t, s], row, 0.0), axis=1, keepdims=True
            )
            divisors.append((own_norms * pivot_norm) * partner_norms[t])

    slots = (G // 2) * NF

    def arrived(k):
        pltpu.make_async_remote_copy(
            src_ref=total.at[0, 0], dst_ref=recv.at[k],
            send_sem=send3.at[0, 0], recv_sem=recv3.at[k],
            device_id=(mate, place), device_id_type=MESH,
        ).wait_recv()

    loop(slots, arrived)
    for s in range(npiv):
        whole = recv[0, s].astype(jnp.float32)
        for k in range(1, slots):
            whole = whole + recv[k, s].astype(jnp.float32)
        for t in range(noff):
            out[t, s] = (
                whole[:, t * rows : (t + 1) * rows] / divisors[t * npiv + s]
            ).astype(out.dtype)

    for sub in range(subs):
        loop(N - 1, lambda k, sub=sub: block_copy(sub, k).wait_send())
    loop(N - 1, lambda k: norm_copy(k).wait_send())
    for g in range(groups):
        mate_copy(g).wait_send()

    def sent(k):
        i, q = k // halves, k % halves

        @pl.when(jnp.logical_not(is_self(i, q)))
        def _():
            total_copy(i, q).wait_send()

    loop(G * halves, sent)


def body(vectors, norms, offsets, pivot_block, pivot_row):
    rows, fields = vectors.shape
    N, NF = lax.axis_size("blk"), lax.axis_size("fld")
    noff, npiv = pivot_block.shape
    G = min(N, fields // LANES)
    C = fields // G
    subs = 2 if C % (2 * LANES) == 0 else 1
    groups = 4
    share = rows // NF
    halves = NF // 2
    wire = jnp.bfloat16 if share % 16 == 0 else jnp.float32
    wide = noff * rows
    slots = (G // 2) * NF
    dims = (N, NF, G, C, subs, groups, rows, noff, npiv)
    dma = pltpu.SemaphoreType.DMA
    smem = pl.BlockSpec(memory_space=pltpu.SMEM)
    vmem = pl.BlockSpec(memory_space=pltpu.VMEM)
    return pl.pallas_call(
        functools.partial(kernel, dims),
        out_shape=jax.ShapeDtypeStruct((noff, npiv, share, rows), jnp.bfloat16),
        in_specs=[smem, smem, smem, pl.BlockSpec(memory_space=pl.ANY), vmem],
        out_specs=vmem,
        scratch_shapes=[
            tuple(pltpu.VMEM((N, rows, C // subs), jnp.bfloat16) for _ in range(subs)),
            pltpu.VMEM((8, LANES), jnp.float32),
            pltpu.VMEM((N, 8, LANES), jnp.float32),
            pltpu.VMEM((noff * npiv, 16, C // subs), jnp.bfloat16),
            pltpu.VMEM((G, 2, halves, npiv, share, wide), jnp.float32),
            pltpu.VMEM((groups, G // groups, halves, npiv, share, wide), wire),
            pltpu.VMEM((groups, G // groups, halves, npiv, share, wide), wire),
            pltpu.VMEM((G, halves, npiv, share, wide), wire),
            pltpu.VMEM((slots, npiv, share, wide), wire),
            dma((subs, N)),
            dma((subs, N)),
            dma((subs,)),
            dma((N,)),
            dma((N,)),
            dma((groups,)),
            dma((groups,)),
            dma((G, halves)),
            dma((slots,)),
        ],
        compiler_params=pltpu.CompilerParams(
            collective_id=0, has_side_effects=True, vmem_limit_bytes=32 * 1024 * 1024
        ),
        cost_estimate=pl.CostEstimate(
            flops=2 * noff * npiv * G * rows * rows * C,
            bytes_accessed=2 * rows * fields * 2,
            transcendentals=0,
        ),
    )(offsets, pivot_block, pivot_row, vectors, norms.reshape(1, rows))


def solution(mesh):
    return jax.shard_map(
        body,
        mesh=mesh,
        in_specs=(P("blk", "fld"), P("blk"), P(), P(), P()),
        out_specs=P(None, None, ("blk", "fld"), None),
        check_vma=False,
    )
```

```python
import functools

import jax
import jax.numpy as jnp
from jax import lax
from jax.experimental import pallas as pl
from jax.experimental.pallas import tpu as pltpu
from jax.sharding import PartitionSpec as P

MESH = pl.DeviceIdType.MESH
LANES = 128


def kernel(
    dims, offsets_in, pivot_block_in, pivot_row_in, vectors, norms_in, out,
    offsets, pivot_block, pivot_row, norms, small, gat, norm_src, norm_all, piv, acc, part, mate_in, total, recv,
    send1, recv1, own1, sendn, recvn, send2, recv2, send3, recv3,
):
    N, NF, G, C, widths, groups, rows, noff, npiv = dims
    share = rows // NF
    halves = NF // 2
    subs = len(widths)
    starts = [sum(widths[:sub]) for sub in range(subs)]
    per = G // groups
    me, place = lax.axis_index("blk"), lax.axis_index("fld")
    group, chunk = me // G, me % G
    base = group * G
    core = me % 2
    mate = me + 1 - 2 * core
    slot = (chunk // 2) * NF + place

    barrier = pltpu.get_barrier_semaphore()

    def greet_blk(j, carry):
        pl.semaphore_signal(
            barrier, inc=1, device_id=(lax.rem(me + j, N), place), device_id_type=MESH
        )
        return carry

    def greet_fld(j, carry):
        other = lax.rem(place + 1 + j // G, NF)
        pl.semaphore_signal(
            barrier, inc=1, device_id=(base + j % G, other), device_id_type=MESH
        )
        return carry

    lax.fori_loop(1, N, greet_blk, 0)
    lax.fori_loop(0, G * (NF - 1), greet_fld, 0)

    smalls = [
        pltpu.make_async_copy(src, dst, small.at[k])
        for k, (src, dst) in enumerate((
            (norms_in, norms), (offsets_in, offsets),
            (pivot_block_in, pivot_block), (pivot_row_in, pivot_row),
        ))
    ]

    def own_copy(sub):
        first = pl.multiple_of(chunk * C + starts[sub], LANES)
        return pltpu.make_async_copy(
            vectors.at[:, pl.ds(first, widths[sub])], gat[sub].at[me], own1.at[sub]
        )

    for copy in smalls:
        copy.start()
    for sub in range(subs):
        own_copy(sub).start()
    norm_src[...] = jnp.zeros_like(norm_src)
    smalls[0].wait()
    norm_src[0:1, 0:rows] = norms[...].astype(jnp.float32)
    norm_all[me] = norm_src[...]
    pl.semaphore_wait(barrier, (N - 1) + G * (NF - 1))

    def shift(k):
        d = (k + 1) // 2
        return N // 2 + d * (2 * (k % 2) - 1)

    def block_copy(sub, k):
        j = shift(k)
        peer = lax.rem(me + j, N)
        first = pl.multiple_of((peer % G) * C + starts[sub], LANES)
        return pltpu.make_async_remote_copy(
            src_ref=vectors.at[:, pl.ds(first, widths[sub])], dst_ref=gat[sub].at[me],
            send_sem=send1.at[sub, j], recv_sem=recv1.at[sub, j],
            device_id=(peer, place), device_id_type=MESH,
        )

    def norm_copy(k):
        j = shift(k)
        peer = lax.rem(me + j, N)
        return pltpu.make_async_remote_copy(
            src_ref=norm_src, dst_ref=norm_all.at[me],
            send_sem=sendn.at[j], recv_sem=recvn.at[j],
            device_id=(peer, place), device_id_type=MESH,
        )

    def loop(count, step):
        def run(k, carry):
            step(k)
            return carry

        lax.fori_loop(0, count, run, 0)

    for sub in range(subs):
        loop(N - 1, lambda k, sub=sub: block_copy(sub, k).start())
    loop(N - 1, lambda k: norm_copy(k).start())

    for copy in smalls[1:]:
        copy.wait()

    def pivots(sub):
        width = widths[sub]
        spot = lax.broadcasted_iota(jnp.int32, (rows, width), 0)
        for t in range(noff):
            for s in range(npiv):
                block = gat[sub][pivot_block[t, s]].astype(jnp.float32)
                picked = jnp.sum(
                    jnp.where(spot == pivot_row[t, s], block, 0.0), axis=0, keepdims=True
                )
                piv[t * npiv + s, :, 0:width] = jnp.broadcast_to(picked, (16, width)).astype(jnp.bfloat16)

    def tile(sub, i):
        block, width = base + i, widths[sub]
        resident = gat[sub][block].reshape(rows // 16, 16, width)
        found = []
        for t in range(noff):
            partner = gat[sub][lax.rem(block + offsets[t], N)]
            scaled = jnp.concatenate(
                [
                    (resident * piv[t * npiv + s, :, 0:width][None]).reshape(rows, width)
                    for s in range(npiv)
                ],
                axis=0,
            )
            found.append(
                lax.dot_general(
                    scaled, partner, (((1,), (1,)), ((), ())),
                    preferred_element_type=jnp.float32,
                )
            )
        value = jnp.concatenate(found, axis=1)
        for s in range(npiv):
            for h in range(NF):
                first = s * rows + h * share
                piece = value[first : first + share]
                if sub > 0:
                    piece = piece + acc[i, h % 2, h // 2, s]
                acc[i, h % 2, h // 2, s] = piece

    def mate_copy(q):
        return pltpu.make_async_remote_copy(
            src_ref=part.at[q], dst_ref=mate_in.at[q],
            send_sem=send2.at[q], recv_sem=recv2.at[q],
            device_id=(mate, place), device_id_type=MESH,
        )

    def total_copy(i, q):
        return pltpu.make_async_remote_copy(
            src_ref=total.at[i, q], dst_ref=recv.at[slot],
            send_sem=send3.at[i, q], recv_sem=recv3.at[slot],
            device_id=(base + i, 2 * q + core), device_id_type=MESH,
        )

    def is_self(i, q):
        return jnp.logical_and(base + i == me, 2 * q + core == place)

    def hand_out(g):
        mate_copy(g).wait_recv()

        def one(k):
            i = g * per + k
            total[i] = (acc[i, core] + mate_in[g, k].astype(jnp.float32)).astype(total.dtype)
            for q in range(halves):
                here = is_self(i, q)

                @pl.when(here)
                def _():
                    pltpu.make_async_copy(total.at[i, q], recv.at[slot], recv3.at[slot]).start()

                @pl.when(jnp.logical_not(here))
                def _():
                    total_copy(i, q).start()

        loop(per, one)

    for sub in range(subs):
        own_copy(sub).wait()
        loop(N - 1, lambda k, sub=sub: block_copy(sub, k).wait_recv())
        pivots(sub)
        if sub < subs - 1:
            def several(g, sub=sub):
                for k in range(per):
                    tile(sub, g * per + k)

            loop(groups, several)
    for g in range(groups):
        for k in range(per):
            tile(subs - 1, g * per + k)
        for k in range(per):
            part[g, k] = acc[g * per + k, 1 - core].astype(part.dtype)
        mate_copy(g).start()
        if g > 0:
            hand_out(g - 1)
    hand_out(groups - 1)

    loop(N - 1, lambda k: norm_copy(k).wait_recv())
    lane = lax.broadcasted_iota(jnp.int32, (1, LANES), 1)
    line = lax.broadcasted_iota(jnp.int32, (share, LANES), 0)
    cols = lax.broadcasted_iota(jnp.int32, (share, LANES), 1)
    own_norms = jnp.sum(
        jnp.where(cols == line + place * share, norm_src[0:1, :], 0.0), axis=1, keepdims=True
    )
    partner_norms = [norm_all[lax.rem(me + offsets[t], N)][0:1, 0:rows] for t in range(noff)]
    divisors = []
    for t in range(noff):
        for s in range(npiv):
            row = norm_all[pivot_block[t, s]][0:1, :]
            pivot_norm = jnp.sum(
                jnp.where(lane == pivot_row[t, s], row, 0.0), axis=1, keepdims=True
            )
            divisors.append((own_norms * pivot_norm) * partner_norms[t])

    slots = (G // 2) * NF

    def arrived(k):
        pltpu.make_async_remote_copy(
            src_ref=total.at[0, 0], dst_ref=recv.at[k],
            send_sem=send3.at[0, 0], recv_sem=recv3.at[k],
            device_id=(mate, place), device_id_type=MESH,
        ).wait_recv()

    loop(slots, arrived)
    for s in range(npiv):
        whole = recv[0, s].astype(jnp.float32)
        for k in range(1, slots):
            whole = whole + recv[k, s].astype(jnp.float32)
        for t in range(noff):
            out[t, s] = (
                whole[:, t * rows : (t + 1) * rows] / divisors[t * npiv + s]
            ).astype(out.dtype)

    for sub in range(subs):
        loop(N - 1, lambda k, sub=sub: block_copy(sub, k).wait_send())
    loop(N - 1, lambda k: norm_copy(k).wait_send())
    for g in range(groups):
        mate_copy(g).wait_send()

    def sent(k):
        i, q = k // halves, k % halves

        @pl.when(jnp.logical_not(is_self(i, q)))
        def _():
            total_copy(i, q).wait_send()

    loop(G * halves, sent)


def body(vectors, norms, offsets, pivot_block, pivot_row):
    rows, fields = vectors.shape
    N, NF = lax.axis_size("blk"), lax.axis_size("fld")
    noff, npiv = pivot_block.shape
    G = min(N, fields // LANES)
    C = fields // G
    widths = (C - LANES, LANES) if C > LANES else (C,)
    groups = 4
    share = rows // NF
    halves = NF // 2
    wire = jnp.bfloat16 if share % 16 == 0 else jnp.float32
    wide = noff * rows
    slots = (G // 2) * NF
    subs = len(widths)
    dims = (N, NF, G, C, widths, groups, rows, noff, npiv)
    dma = pltpu.SemaphoreType.DMA
    anywhere = pl.BlockSpec(memory_space=pl.ANY)
    return pl.pallas_call(
        functools.partial(kernel, dims),
        out_shape=jax.ShapeDtypeStruct((noff, npiv, share, rows), jnp.bfloat16),
        in_specs=[anywhere] * 5,
        out_specs=pl.BlockSpec(memory_space=pltpu.VMEM),
        scratch_shapes=[
            pltpu.SMEM(offsets.shape, jnp.int32),
            pltpu.SMEM(pivot_block.shape, jnp.int32),
            pltpu.SMEM(pivot_row.shape, jnp.int32),
            pltpu.VMEM((1, rows), jnp.bfloat16),
            dma((4,)),
            tuple(pltpu.VMEM((N, rows, width), jnp.bfloat16) for width in widths),
            pltpu.VMEM((8, LANES), jnp.float32),
            pltpu.VMEM((N, 8, LANES), jnp.float32),
            pltpu.VMEM((noff * npiv, 16, max(widths)), jnp.bfloat16),
            pltpu.VMEM((G, 2, halves, npiv, share, wide), jnp.float32),
            pltpu.VMEM((groups, G // groups, halves, npiv, share, wide), wire),
            pltpu.VMEM((groups, G // groups, halves, npiv, share, wide), wire),
            pltpu.VMEM((G, halves, npiv, share, wide), wire),
            pltpu.VMEM((slots, npiv, share, wide), wire),
            dma((subs, N)),
            dma((subs, N)),
            dma((subs,)),
            dma((N,)),
            dma((N,)),
            dma((groups,)),
            dma((groups,)),
            dma((G, halves)),
            dma((slots,)),
        ],
        compiler_params=pltpu.CompilerParams(
            collective_id=0, has_side_effects=True, vmem_limit_bytes=63 * 1024 * 1024
        ),
        cost_estimate=pl.CostEstimate(
            flops=2 * noff * npiv * G * rows * rows * C,
            bytes_accessed=2 * rows * fields * 2,
            transcendentals=0,
        ),
    )(offsets, pivot_block, pivot_row, vectors, norms.reshape(1, rows))


def solution(mesh):
    return jax.shard_map(
        body,
        mesh=mesh,
        in_specs=(P("blk", "fld"), P("blk"), P(), P(), P()),
        out_specs=P(None, None, ("blk", "fld"), None),
        check_vma=False,
    )
```

```python
import functools

import jax
import jax.numpy as jnp
from jax import lax
from jax.experimental import pallas as pl
from jax.experimental.pallas import tpu as pltpu
from jax.sharding import PartitionSpec as P

MESH = pl.DeviceIdType.MESH
LANES = 128


def kernel(
    dims, offsets_in, pivot_block_in, pivot_row_in, vectors, norms_in, out,
    offsets, pivot_block, pivot_row, norms, small, gat, norm_src, norm_all, piv, acc, part, mate_in, total, recv,
    send1, recv1, own1, sendn, recvn, send2, recv2, send3, recv3,
):
    N, NF, G, C, widths, groups, rows, noff, npiv = dims
    share = rows // NF
    halves = NF // 2
    subs = len(widths)
    starts = [sum(widths[:sub]) for sub in range(subs)]
    per = G // groups
    me, place = lax.axis_index("blk"), lax.axis_index("fld")
    group, chunk = me // G, me % G
    base = group * G
    core = me % 2
    mate = me + 1 - 2 * core
    slot = (chunk // 2) * NF + place

    barrier = pltpu.get_barrier_semaphore()

    def greet_blk(j, carry):
        pl.semaphore_signal(
            barrier, inc=1, device_id=(lax.rem(me + j, N), place), device_id_type=MESH
        )
        return carry

    def greet_fld(j, carry):
        other = lax.rem(place + 1 + j // G, NF)
        pl.semaphore_signal(
            barrier, inc=1, device_id=(base + j % G, other), device_id_type=MESH
        )
        return carry

    lax.fori_loop(1, N, greet_blk, 0)
    lax.fori_loop(0, G * (NF - 1), greet_fld, 0)

    smalls = [
        pltpu.make_async_copy(src, dst, small.at[k])
        for k, (src, dst) in enumerate((
            (norms_in, norms), (offsets_in, offsets),
            (pivot_block_in, pivot_block), (pivot_row_in, pivot_row),
        ))
    ]

    def own_copy(sub):
        first = pl.multiple_of(chunk * C + starts[sub], LANES)
        return pltpu.make_async_copy(
            vectors.at[:, pl.ds(first, widths[sub])], gat[sub].at[me], own1.at[sub]
        )

    for copy in smalls:
        copy.start()
    for sub in range(subs):
        own_copy(sub).start()
    norm_src[...] = jnp.zeros_like(norm_src)
    smalls[0].wait()
    norm_src[0:1, 0:rows] = norms[...].astype(jnp.float32)
    norm_all[me] = norm_src[...]
    pl.semaphore_wait(barrier, (N - 1) + G * (NF - 1))

    side = N // 2

    def peer_of(k):
        half, spot = me // side, me % side
        other = k % 2 == 0
        turn = lax.rem(spot + (k + 1) // 2, side)
        return jnp.where(other, 1 - half, half) * side + turn

    def block_copy(sub, k):
        peer = peer_of(k)
        first = pl.multiple_of((peer % G) * C + starts[sub], LANES)
        return pltpu.make_async_remote_copy(
            src_ref=vectors.at[:, pl.ds(first, widths[sub])], dst_ref=gat[sub].at[me],
            send_sem=send1.at[sub, k], recv_sem=recv1.at[sub, k],
            device_id=(peer, place), device_id_type=MESH,
        )

    def norm_copy(k):
        return pltpu.make_async_remote_copy(
            src_ref=norm_src, dst_ref=norm_all.at[me],
            send_sem=sendn.at[k], recv_sem=recvn.at[k],
            device_id=(peer_of(k), place), device_id_type=MESH,
        )

    def loop(count, step):
        def run(k, carry):
            step(k)
            return carry

        lax.fori_loop(0, count, run, 0)

    for sub in range(subs):
        loop(N - 1, lambda k, sub=sub: block_copy(sub, k).start())
    loop(N - 1, lambda k: norm_copy(k).start())

    for copy in smalls[1:]:
        copy.wait()

    def pivots(sub):
        width = widths[sub]
        spot = lax.broadcasted_iota(jnp.int32, (rows, width), 0)
        for t in range(noff):
            for s in range(npiv):
                block = gat[sub][pivot_block[t, s]].astype(jnp.float32)
                picked = jnp.sum(
                    jnp.where(spot == pivot_row[t, s], block, 0.0), axis=0, keepdims=True
                )
                piv[t * npiv + s, :, 0:width] = jnp.broadcast_to(picked, (16, width)).astype(jnp.bfloat16)

    def tile(sub, i):
        block, width = base + i, widths[sub]
        resident = gat[sub][block].reshape(rows // 16, 16, width)
        found = []
        for t in range(noff):
            partner = gat[sub][lax.rem(block + offsets[t], N)]
            scaled = jnp.concatenate(
                [
                    (resident * piv[t * npiv + s, :, 0:width][None]).reshape(rows, width)
                    for s in range(npiv)
                ],
                axis=0,
            )
            found.append(
                lax.dot_general(
                    scaled, partner, (((1,), (1,)), ((), ())),
                    preferred_element_type=jnp.float32,
                )
            )
        value = jnp.concatenate(found, axis=1)
        for s in range(npiv):
            for h in range(NF):
                first = s * rows + h * share
                piece = value[first : first + share]
                if sub > 0:
                    piece = piece + acc[i, h % 2, h // 2, s]
                acc[i, h % 2, h // 2, s] = piece

    def mate_copy(q):
        return pltpu.make_async_remote_copy(
            src_ref=part.at[q], dst_ref=mate_in.at[q],
            send_sem=send2.at[q], recv_sem=recv2.at[q],
            device_id=(mate, place), device_id_type=MESH,
        )

    def total_copy(i, q):
        return pltpu.make_async_remote_copy(
            src_ref=total.at[i, q], dst_ref=recv.at[slot],
            send_sem=send3.at[i, q], recv_sem=recv3.at[slot],
            device_id=(base + i, 2 * q + core), device_id_type=MESH,
        )

    def is_self(i, q):
        return jnp.logical_and(base + i == me, 2 * q + core == place)

    def hand_out(g):
        mate_copy(g).wait_recv()

        def one(k):
            i = g * per + k
            total[i] = (acc[i, core] + mate_in[g, k].astype(jnp.float32)).astype(total.dtype)
            for q in range(halves):
                here = is_self(i, q)

                @pl.when(here)
                def _():
                    pltpu.make_async_copy(total.at[i, q], recv.at[slot], recv3.at[slot]).start()

                @pl.when(jnp.logical_not(here))
                def _():
                    total_copy(i, q).start()

        loop(per, one)

    for sub in range(subs):
        own_copy(sub).wait()
        loop(N - 1, lambda k, sub=sub: block_copy(sub, k).wait_recv())
        pivots(sub)
        if sub < subs - 1:
            def several(g, sub=sub):
                for k in range(per):
                    tile(sub, g * per + k)

            loop(groups, several)
    for g in range(groups):
        for k in range(per):
            tile(subs - 1, g * per + k)
        for k in range(per):
            part[g, k] = acc[g * per + k, 1 - core].astype(part.dtype)
        mate_copy(g).start()
        if g > 0:
            hand_out(g - 1)
    hand_out(groups - 1)

    loop(N - 1, lambda k: norm_copy(k).wait_recv())
    lane = lax.broadcasted_iota(jnp.int32, (1, LANES), 1)
    line = lax.broadcasted_iota(jnp.int32, (share, LANES), 0)
    cols = lax.broadcasted_iota(jnp.int32, (share, LANES), 1)
    own_norms = jnp.sum(
        jnp.where(cols == line + place * share, norm_src[0:1, :], 0.0), axis=1, keepdims=True
    )
    partner_norms = [norm_all[lax.rem(me + offsets[t], N)][0:1, 0:rows] for t in range(noff)]
    divisors = []
    for t in range(noff):
        for s in range(npiv):
            row = norm_all[pivot_block[t, s]][0:1, :]
            pivot_norm = jnp.sum(
                jnp.where(lane == pivot_row[t, s], row, 0.0), axis=1, keepdims=True
            )
            divisors.append((own_norms * pivot_norm) * partner_norms[t])

    slots = (G // 2) * NF

    def arrived(k):
        pltpu.make_async_remote_copy(
            src_ref=total.at[0, 0], dst_ref=recv.at[k],
            send_sem=send3.at[0, 0], recv_sem=recv3.at[k],
            device_id=(mate, place), device_id_type=MESH,
        ).wait_recv()

    loop(slots, arrived)
    for s in range(npiv):
        whole = recv[0, s].astype(jnp.float32)
        for k in range(1, slots):
            whole = whole + recv[k, s].astype(jnp.float32)
        for t in range(noff):
            out[t, s] = (
                whole[:, t * rows : (t + 1) * rows] / divisors[t * npiv + s]
            ).astype(out.dtype)

    for sub in range(subs):
        loop(N - 1, lambda k, sub=sub: block_copy(sub, k).wait_send())
    loop(N - 1, lambda k: norm_copy(k).wait_send())
    for g in range(groups):
        mate_copy(g).wait_send()

    def sent(k):
        i, q = k // halves, k % halves

        @pl.when(jnp.logical_not(is_self(i, q)))
        def _():
            total_copy(i, q).wait_send()

    loop(G * halves, sent)


def body(vectors, norms, offsets, pivot_block, pivot_row):
    rows, fields = vectors.shape
    N, NF = lax.axis_size("blk"), lax.axis_size("fld")
    noff, npiv = pivot_block.shape
    G = min(N, fields // LANES)
    C = fields // G
    widths = (C - LANES, LANES) if C > LANES else (C,)
    groups = 4
    share = rows // NF
    halves = NF // 2
    wire = jnp.bfloat16 if share % 16 == 0 else jnp.float32
    wide = noff * rows
    slots = (G // 2) * NF
    subs = len(widths)
    dims = (N, NF, G, C, widths, groups, rows, noff, npiv)
    dma = pltpu.SemaphoreType.DMA
    anywhere = pl.BlockSpec(memory_space=pl.ANY)
    return pl.pallas_call(
        functools.partial(kernel, dims),
        out_shape=jax.ShapeDtypeStruct((noff, npiv, share, rows), jnp.bfloat16),
        in_specs=[anywhere] * 5,
        out_specs=pl.BlockSpec(memory_space=pltpu.VMEM),
        scratch_shapes=[
            pltpu.SMEM(offsets.shape, jnp.int32),
            pltpu.SMEM(pivot_block.shape, jnp.int32),
            pltpu.SMEM(pivot_row.shape, jnp.int32),
            pltpu.VMEM((1, rows), jnp.bfloat16),
            dma((4,)),
            tuple(pltpu.VMEM((N, rows, width), jnp.bfloat16) for width in widths),
            pltpu.VMEM((8, LANES), jnp.float32),
            pltpu.VMEM((N, 8, LANES), jnp.float32),
            pltpu.VMEM((noff * npiv, 16, max(widths)), jnp.bfloat16),
            pltpu.VMEM((G, 2, halves, npiv, share, wide), jnp.float32),
            pltpu.VMEM((groups, G // groups, halves, npiv, share, wide), wire),
            pltpu.VMEM((groups, G // groups, halves, npiv, share, wide), wire),
            pltpu.VMEM((G, halves, npiv, share, wide), wire),
            pltpu.VMEM((slots, npiv, share, wide), wire),
            dma((subs, N)),
            dma((subs, N)),
            dma((subs,)),
            dma((N,)),
            dma((N,)),
            dma((groups,)),
            dma((groups,)),
            dma((G, halves)),
            dma((slots,)),
        ],
        compiler_params=pltpu.CompilerParams(
            collective_id=0, has_side_effects=True, vmem_limit_bytes=63 * 1024 * 1024
        ),
        cost_estimate=pl.CostEstimate(
            flops=2 * noff * npiv * G * rows * rows * C,
            bytes_accessed=2 * rows * fields * 2,
            transcendentals=0,
        ),
    )(offsets, pivot_block, pivot_row, vectors, norms.reshape(1, rows))


def solution(mesh):
    return jax.shard_map(
        body,
        mesh=mesh,
        in_specs=(P("blk", "fld"), P("blk"), P(), P(), P()),
        out_specs=P(None, None, ("blk", "fld"), None),
        check_vma=False,
    )
```

```python
import functools

import jax
import jax.numpy as jnp
from jax import lax
from jax.experimental import pallas as pl
from jax.experimental.pallas import tpu as pltpu
from jax.sharding import PartitionSpec as P

MESH = pl.DeviceIdType.MESH
LANES = 128


def kernel(
    dims, offsets_in, pivot_block_in, pivot_row_in, vectors, norms_in, out,
    offsets, pivot_block, pivot_row, norms, small, gat, norm_src, norm_all, piv, acc, part, mate_in, total, cross_in, final, recv,
    send1, recv1, own1, sendn, recvn, send2, recv2, sendx, recvx, send3, recv3,
):
    N, NF, G, C, widths, groups, rows, noff, npiv = dims
    share = rows // NF
    halves = NF // 2
    subs = len(widths)
    starts = [sum(widths[:sub]) for sub in range(subs)]
    per = G // groups
    me, place = lax.axis_index("blk"), lax.axis_index("fld")
    group, chunk = me // G, me % G
    base = group * G
    core = me % 2
    mate = me + 1 - 2 * core
    slot = chunk // 2
    gathers = place % 2 == core

    barrier = pltpu.get_barrier_semaphore()

    def greet_blk(j, carry):
        pl.semaphore_signal(
            barrier, inc=1, device_id=(lax.rem(me + j, N), place), device_id_type=MESH
        )
        return carry

    def greet_fld(j, carry):
        pl.semaphore_signal(
            barrier, inc=1, device_id=(me, lax.rem(place + j, NF)), device_id_type=MESH
        )
        return carry

    lax.fori_loop(1, N, greet_blk, 0)
    lax.fori_loop(1, NF, greet_fld, 0)

    smalls = [
        pltpu.make_async_copy(src, dst, small.at[k])
        for k, (src, dst) in enumerate((
            (norms_in, norms), (offsets_in, offsets),
            (pivot_block_in, pivot_block), (pivot_row_in, pivot_row),
        ))
    ]

    def own_copy(sub):
        first = pl.multiple_of(chunk * C + starts[sub], LANES)
        return pltpu.make_async_copy(
            vectors.at[:, pl.ds(first, widths[sub])], gat[sub].at[me], own1.at[sub]
        )

    for copy in smalls:
        copy.start()
    for sub in range(subs):
        own_copy(sub).start()
    norm_src[...] = jnp.zeros_like(norm_src)
    smalls[0].wait()
    norm_src[0:1, 0:rows] = norms[...].astype(jnp.float32)
    norm_all[me] = norm_src[...]
    pl.semaphore_wait(barrier, (N - 1) + (NF - 1))

    side = N // 2

    def peer_of(k):
        half, spot = me // side, me % side
        other = k % 2 == 0
        turn = lax.rem(spot + (k + 1) // 2, side)
        return jnp.where(other, 1 - half, half) * side + turn

    def block_copy(sub, k):
        peer = peer_of(k)
        first = pl.multiple_of((peer % G) * C + starts[sub], LANES)
        return pltpu.make_async_remote_copy(
            src_ref=vectors.at[:, pl.ds(first, widths[sub])], dst_ref=gat[sub].at[me],
            send_sem=send1.at[sub, k], recv_sem=recv1.at[sub, k],
            device_id=(peer, place), device_id_type=MESH,
        )

    def norm_copy(k):
        return pltpu.make_async_remote_copy(
            src_ref=norm_src, dst_ref=norm_all.at[me],
            send_sem=sendn.at[k], recv_sem=recvn.at[k],
            device_id=(peer_of(k), place), device_id_type=MESH,
        )

    def loop(count, step):
        def run(k, carry):
            step(k)
            return carry

        lax.fori_loop(0, count, run, 0)

    for sub in range(subs):
        loop(N - 1, lambda k, sub=sub: block_copy(sub, k).start())
    loop(N - 1, lambda k: norm_copy(k).start())

    for copy in smalls[1:]:
        copy.wait()

    def pivots(sub):
        width = widths[sub]
        spot = lax.broadcasted_iota(jnp.int32, (rows, width), 0)
        for t in range(noff):
            for s in range(npiv):
                block = gat[sub][pivot_block[t, s]].astype(jnp.float32)
                picked = jnp.sum(
                    jnp.where(spot == pivot_row[t, s], block, 0.0), axis=0, keepdims=True
                )
                piv[t * npiv + s, :, 0:width] = jnp.broadcast_to(picked, (16, width)).astype(jnp.bfloat16)

    def index(g, k):
        return k * groups + (g + (groups // 2) * (k % 2)) % groups

    def tile(sub, g, k):
        block, width = base + index(g, k), widths[sub]
        resident = gat[sub][block].reshape(rows // 16, 16, width)
        found = []
        for t in range(noff):
            partner = gat[sub][lax.rem(block + offsets[t], N)]
            scaled = jnp.concatenate(
                [
                    (resident * piv[t * npiv + s, :, 0:width][None]).reshape(rows, width)
                    for s in range(npiv)
                ],
                axis=0,
            )
            found.append(
                lax.dot_general(
                    scaled, partner, (((1,), (1,)), ((), ())),
                    preferred_element_type=jnp.float32,
                )
            )
        value = jnp.concatenate(found, axis=1)
        for s in range(npiv):
            for h in range(NF):
                first = s * rows + h * share
                piece = value[first : first + share]
                if sub > 0:
                    piece = piece + acc[g, k, h % 2, h // 2, s]
                acc[g, k, h % 2, h // 2, s] = piece

    def mate_copy(q):
        return pltpu.make_async_remote_copy(
            src_ref=part.at[q], dst_ref=mate_in.at[q],
            send_sem=send2.at[q], recv_sem=recv2.at[q],
            device_id=(mate, place), device_id_type=MESH,
        )

    def cross_copy(g, q):
        target = 2 * q + core
        lane = lax.rem(place - target + NF, NF) - 1
        return pltpu.make_async_remote_copy(
            src_ref=total.at[g, q], dst_ref=cross_in.at[g, lane],
            send_sem=sendx.at[g, q], recv_sem=recvx.at[g, lane],
            device_id=(me, target), device_id_type=MESH,
        )

    def cross_arrival(g, lane):
        return pltpu.make_async_remote_copy(
            src_ref=total.at[g, 0], dst_ref=cross_in.at[g, lane],
            send_sem=sendx.at[g, 0], recv_sem=recvx.at[g, lane],
            device_id=(me, lax.rem(place + 1, NF)), device_id_type=MESH,
        )

    def final_copy(g, k):
        return pltpu.make_async_remote_copy(
            src_ref=final.at[g, k], dst_ref=recv.at[slot],
            send_sem=send3.at[g, k], recv_sem=recv3.at[slot],
            device_id=(base + index(g, k), place), device_id_type=MESH,
        )

    def over_fld(g):
        mate_copy(g).wait_recv()
        for q in range(halves):
            @pl.when(2 * q + core != place)
            def _():
                for k in range(per):
                    total[g, q, k] = (
                        acc[g, k, core, q] + mate_in[g, k, q].astype(jnp.float32)
                    ).astype(total.dtype)
                cross_copy(g, q).start()

    def over_blk(g):
        @pl.when(gathers)
        def _():
            for lane in range(NF - 1):
                cross_arrival(g, lane).wait_recv()
            for k in range(per):
                whole = acc[g, k, core, place // 2] + mate_in[g, k, place // 2].astype(jnp.float32)
                for lane in range(NF - 1):
                    whole = whole + cross_in[g, lane, k].astype(jnp.float32)
                final[g, k] = whole.astype(final.dtype)
                here = base + index(g, k) == me

                @pl.when(here)
                def _():
                    pltpu.make_async_copy(final.at[g, k], recv.at[slot], recv3.at[slot]).start()

                @pl.when(jnp.logical_not(here))
                def _():
                    final_copy(g, k).start()

    for sub in range(subs):
        own_copy(sub).wait()
        loop(N - 1, lambda k, sub=sub: block_copy(sub, k).wait_recv())
        pivots(sub)
        if sub < subs - 1:
            def several(g, sub=sub):
                for k in range(per):
                    tile(sub, g, k)

            loop(groups, several)
    for g in range(groups):
        for k in range(per):
            tile(subs - 1, g, k)
        for k in range(per):
            part[g, k] = acc[g, k, 1 - core].astype(part.dtype)
        mate_copy(g).start()
        if g > 0:
            over_fld(g - 1)
        if g > 1:
            over_blk(g - 2)
    over_fld(groups - 1)
    if groups > 1:
        over_blk(groups - 2)
    over_blk(groups - 1)

    loop(N - 1, lambda k: norm_copy(k).wait_recv())
    lane = lax.broadcasted_iota(jnp.int32, (1, LANES), 1)
    line = lax.broadcasted_iota(jnp.int32, (share, LANES), 0)
    cols = lax.broadcasted_iota(jnp.int32, (share, LANES), 1)
    own_norms = jnp.sum(
        jnp.where(cols == line + place * share, norm_src[0:1, :], 0.0), axis=1, keepdims=True
    )
    partner_norms = [norm_all[lax.rem(me + offsets[t], N)][0:1, 0:rows] for t in range(noff)]
    divisors = []
    for t in range(noff):
        for s in range(npiv):
            row = norm_all[pivot_block[t, s]][0:1, :]
            pivot_norm = jnp.sum(
                jnp.where(lane == pivot_row[t, s], row, 0.0), axis=1, keepdims=True
            )
            divisors.append((own_norms * pivot_norm) * partner_norms[t])

    slots = G // 2

    def arrived(k):
        pltpu.make_async_remote_copy(
            src_ref=final.at[0, 0], dst_ref=recv.at[k],
            send_sem=send3.at[0, 0], recv_sem=recv3.at[k],
            device_id=(mate, place), device_id_type=MESH,
        ).wait_recv()

    loop(slots, arrived)
    for s in range(npiv):
        whole = recv[0, s].astype(jnp.float32)
        for k in range(1, slots):
            whole = whole + recv[k, s].astype(jnp.float32)
        for t in range(noff):
            out[t, s] = (
                whole[:, t * rows : (t + 1) * rows] / divisors[t * npiv + s]
            ).astype(out.dtype)

    for sub in range(subs):
        loop(N - 1, lambda k, sub=sub: block_copy(sub, k).wait_send())
    loop(N - 1, lambda k: norm_copy(k).wait_send())
    for g in range(groups):
        mate_copy(g).wait_send()

    for g in range(groups):
        for q in range(halves):
            @pl.when(2 * q + core != place)
            def _():
                cross_copy(g, q).wait_send()

    def sent(j):
        g, k = j // per, j % per

        @pl.when(base + index(g, k) != me)
        def _():
            final_copy(g, k).wait_send()

    @pl.when(gathers)
    def _():
        loop(G, sent)


def body(vectors, norms, offsets, pivot_block, pivot_row):
    rows, fields = vectors.shape
    N, NF = lax.axis_size("blk"), lax.axis_size("fld")
    noff, npiv = pivot_block.shape
    G = min(N, fields // LANES)
    C = fields // G
    widths = (C - LANES, LANES) if C > LANES else (C,)
    groups = 4 if G % 4 == 0 else 1
    per = G // groups
    share = rows // NF
    halves = NF // 2
    wire = jnp.bfloat16 if share % 16 == 0 else jnp.float32
    wide = noff * rows
    slots = G // 2
    subs = len(widths)
    dims = (N, NF, G, C, widths, groups, rows, noff, npiv)
    dma = pltpu.SemaphoreType.DMA
    anywhere = pl.BlockSpec(memory_space=pl.ANY)
    return pl.pallas_call(
        functools.partial(kernel, dims),
        out_shape=jax.ShapeDtypeStruct((noff, npiv, share, rows), jnp.bfloat16),
        in_specs=[anywhere] * 5,
        out_specs=pl.BlockSpec(memory_space=pltpu.VMEM),
        scratch_shapes=[
            pltpu.SMEM(offsets.shape, jnp.int32),
            pltpu.SMEM(pivot_block.shape, jnp.int32),
            pltpu.SMEM(pivot_row.shape, jnp.int32),
            pltpu.VMEM((1, rows), jnp.bfloat16),
            dma((4,)),
            tuple(pltpu.VMEM((N, rows, width), jnp.bfloat16) for width in widths),
            pltpu.VMEM((8, LANES), jnp.float32),
            pltpu.VMEM((N, 8, LANES), jnp.float32),
            pltpu.VMEM((noff * npiv, 16, max(widths)), jnp.bfloat16),
            pltpu.VMEM((groups, per, 2, halves, npiv, share, wide), jnp.float32),
            pltpu.VMEM((groups, per, halves, npiv, share, wide), wire),
            pltpu.VMEM((groups, per, halves, npiv, share, wide), wire),
            pltpu.VMEM((groups, halves, per, npiv, share, wide), wire),
            pltpu.VMEM((groups, NF - 1, per, npiv, share, wide), wire),
            pltpu.VMEM((groups, per, npiv, share, wide), wire),
            pltpu.VMEM((slots, npiv, share, wide), wire),
            dma((subs, N)),
            dma((subs, N)),
            dma((subs,)),
            dma((N,)),
            dma((N,)),
            dma((groups,)),
            dma((groups,)),
            dma((groups, halves)),
            dma((groups, NF - 1)),
            dma((groups, per)),
            dma((slots,)),
        ],
        compiler_params=pltpu.CompilerParams(
            collective_id=0, has_side_effects=True, vmem_limit_bytes=63 * 1024 * 1024
        ),
        cost_estimate=pl.CostEstimate(
            flops=2 * noff * npiv * G * rows * rows * C,
            bytes_accessed=2 * rows * fields * 2,
            transcendentals=0,
        ),
    )(offsets, pivot_block, pivot_row, vectors, norms.reshape(1, rows))


def solution(mesh):
    return jax.shard_map(
        body,
        mesh=mesh,
        in_specs=(P("blk", "fld"), P("blk"), P(), P(), P()),
        out_specs=P(None, None, ("blk", "fld"), None),
        check_vma=False,
    )
```

```python
import functools

import jax
import jax.numpy as jnp
from jax import lax
from jax.experimental import pallas as pl
from jax.experimental.pallas import tpu as pltpu
from jax.sharding import PartitionSpec as P

MESH = pl.DeviceIdType.MESH
LANES = 128


def kernel(
    dims, offsets_in, pivot_block_in, pivot_row_in, vectors, norms_in, out,
    offsets, pivot_block, pivot_row, norms, small, gat, norm_src, norm_all, piv, acc, part, mate_in, total, cross_in, final, recv,
    send1, recv1, own1, sendn, recvn, send2, recv2, sendx, recvx, send3, recv3,
):
    N, NF, G, C, widths, groups, rows, noff, npiv = dims
    share = rows // NF
    halves = NF // 2
    subs = len(widths)
    starts = [sum(widths[:sub]) for sub in range(subs)]
    per = G // groups
    me, place = lax.axis_index("blk"), lax.axis_index("fld")
    group, chunk = me // G, me % G
    base = group * G
    core = me % 2
    mate = me + 1 - 2 * core
    slot = chunk // 2
    gathers = place % 2 == core

    barrier = pltpu.get_barrier_semaphore()

    def greet_blk(j, carry):
        pl.semaphore_signal(
            barrier, inc=1, device_id=(lax.rem(me + j, N), place), device_id_type=MESH
        )
        return carry

    def greet_fld(j, carry):
        pl.semaphore_signal(
            barrier, inc=1, device_id=(me, lax.rem(place + j, NF)), device_id_type=MESH
        )
        return carry

    lax.fori_loop(1, N, greet_blk, 0)
    lax.fori_loop(1, NF, greet_fld, 0)

    smalls = [
        pltpu.make_async_copy(src, dst, small.at[k])
        for k, (src, dst) in enumerate((
            (norms_in, norms), (offsets_in, offsets),
            (pivot_block_in, pivot_block), (pivot_row_in, pivot_row),
        ))
    ]

    def own_copy(sub):
        first = pl.multiple_of(chunk * C + starts[sub], LANES)
        return pltpu.make_async_copy(
            vectors.at[:, pl.ds(first, widths[sub])], gat[sub].at[me], own1.at[sub]
        )

    for copy in smalls:
        copy.start()
    for sub in range(subs):
        own_copy(sub).start()
    norm_src[...] = jnp.zeros_like(norm_src)
    smalls[0].wait()
    norm_src[0:1, 0:rows] = norms[...].astype(jnp.float32)
    norm_all[me] = norm_src[...]
    pl.semaphore_wait(barrier, (N - 1) + (NF - 1))

    side = N // 2

    def peer_of(k):
        half, spot = me // side, me % side
        other = k % 2 == 0
        turn = lax.rem(spot + (k + 1) // 2, side)
        return jnp.where(other, 1 - half, half) * side + turn

    def block_copy(sub, k):
        peer = peer_of(k)
        first = pl.multiple_of((peer % G) * C + starts[sub], LANES)
        return pltpu.make_async_remote_copy(
            src_ref=vectors.at[:, pl.ds(first, widths[sub])], dst_ref=gat[sub].at[me],
            send_sem=send1.at[sub, k], recv_sem=recv1.at[sub, k],
            device_id=(peer, place), device_id_type=MESH,
        )

    def norm_copy(k):
        return pltpu.make_async_remote_copy(
            src_ref=norm_src, dst_ref=norm_all.at[me],
            send_sem=sendn.at[k], recv_sem=recvn.at[k],
            device_id=(peer_of(k), place), device_id_type=MESH,
        )

    def loop(count, step):
        def run(k, carry):
            step(k)
            return carry

        lax.fori_loop(0, count, run, 0)

    for sub in range(subs):
        loop(N - 1, lambda k, sub=sub: block_copy(sub, k).start())
    loop(N - 1, lambda k: norm_copy(k).start())

    for copy in smalls[1:]:
        copy.wait()

    def pivots(sub):
        width = widths[sub]
        spot = lax.broadcasted_iota(jnp.int32, (rows, width), 0)
        for t in range(noff):
            for s in range(npiv):
                block = gat[sub][pivot_block[t, s]].astype(jnp.float32)
                picked = jnp.sum(
                    jnp.where(spot == pivot_row[t, s], block, 0.0), axis=0, keepdims=True
                )
                piv[t * npiv + s, :, 0:width] = jnp.broadcast_to(picked, (16, width)).astype(jnp.bfloat16)

    def index(g, k):
        return k * groups + (g + (groups // 2) * (k % 2)) % groups

    def tile(sub, g, k):
        block, width = base + index(g, k), widths[sub]
        resident = gat[sub][block].reshape(rows // 16, 16, width)
        ahead = [block + offsets[t] for t in range(noff)]
        partner = jnp.concatenate(
            [gat[sub][jnp.where(b < N, b, b - N)] for b in ahead], axis=0
        )
        scaled = jnp.concatenate(
            [
                (resident * piv[j, :, 0:width][None]).reshape(rows, width)
                for j in range(noff * npiv)
            ],
            axis=0,
        )
        met = lax.dot_general(
            scaled, partner, (((1,), (1,)), ((), ())), preferred_element_type=jnp.float32
        )
        lane = lax.broadcasted_iota(jnp.int32, (npiv * rows, noff * rows), 1)
        value = met[0 : npiv * rows]
        for t in range(1, noff):
            value = jnp.where(
                lane < t * rows, value, met[t * npiv * rows : (t + 1) * npiv * rows]
            )
        for s in range(npiv):
            for h in range(NF):
                first = s * rows + h * share
                piece = value[first : first + share]
                if sub > 0:
                    piece = piece + acc[g, k, h % 2, h // 2, s]
                acc[g, k, h % 2, h // 2, s] = piece

    def mate_copy(q):
        return pltpu.make_async_remote_copy(
            src_ref=part.at[q], dst_ref=mate_in.at[q],
            send_sem=send2.at[q], recv_sem=recv2.at[q],
            device_id=(mate, place), device_id_type=MESH,
        )

    def cross_copy(g, q):
        target = 2 * q + core
        lane = lax.rem(place - target + NF, NF) - 1
        return pltpu.make_async_remote_copy(
            src_ref=total.at[g, q], dst_ref=cross_in.at[g, lane],
            send_sem=sendx.at[g, q], recv_sem=recvx.at[g, lane],
            device_id=(me, target), device_id_type=MESH,
        )

    def cross_arrival(g, lane):
        return pltpu.make_async_remote_copy(
            src_ref=total.at[g, 0], dst_ref=cross_in.at[g, lane],
            send_sem=sendx.at[g, 0], recv_sem=recvx.at[g, lane],
            device_id=(me, lax.rem(place + 1, NF)), device_id_type=MESH,
        )

    def final_copy(g, k):
        return pltpu.make_async_remote_copy(
            src_ref=final.at[g, k], dst_ref=recv.at[slot],
            send_sem=send3.at[g, k], recv_sem=recv3.at[slot],
            device_id=(base + index(g, k), place), device_id_type=MESH,
        )

    def over_fld(g):
        mate_copy(g).wait_recv()
        for q in range(halves):
            @pl.when(2 * q + core != place)
            def _():
                for k in range(per):
                    total[g, q, k] = (
                        acc[g, k, core, q] + mate_in[g, k, q].astype(jnp.float32)
                    ).astype(total.dtype)
                cross_copy(g, q).start()

    def over_blk(g):
        @pl.when(gathers)
        def _():
            for lane in range(NF - 1):
                cross_arrival(g, lane).wait_recv()
            for k in range(per):
                whole = acc[g, k, core, place // 2] + mate_in[g, k, place // 2].astype(jnp.float32)
                for lane in range(NF - 1):
                    whole = whole + cross_in[g, lane, k].astype(jnp.float32)
                final[g, k] = whole.astype(final.dtype)
                here = base + index(g, k) == me

                @pl.when(here)
                def _():
                    pltpu.make_async_copy(final.at[g, k], recv.at[slot], recv3.at[slot]).start()

                @pl.when(jnp.logical_not(here))
                def _():
                    final_copy(g, k).start()

    for sub in range(subs):
        own_copy(sub).wait()
        loop(N - 1, lambda k, sub=sub: block_copy(sub, k).wait_recv())
        pivots(sub)
        if sub < subs - 1:
            def several(g, sub=sub):
                for k in range(per):
                    tile(sub, g, k)

            loop(groups, several)
    for g in range(groups):
        for k in range(per):
            tile(subs - 1, g, k)
        for k in range(per):
            part[g, k] = acc[g, k, 1 - core].astype(part.dtype)
        mate_copy(g).start()
        if g > 0:
            over_fld(g - 1)
        if g > 1:
            over_blk(g - 2)
    over_fld(groups - 1)
    if groups > 1:
        over_blk(groups - 2)
    over_blk(groups - 1)

    loop(N - 1, lambda k: norm_copy(k).wait_recv())
    lane = lax.broadcasted_iota(jnp.int32, (1, LANES), 1)
    line = lax.broadcasted_iota(jnp.int32, (share, LANES), 0)
    cols = lax.broadcasted_iota(jnp.int32, (share, LANES), 1)
    own_norms = jnp.sum(
        jnp.where(cols == line + place * share, norm_src[0:1, :], 0.0), axis=1, keepdims=True
    )
    partner_norms = [norm_all[lax.rem(me + offsets[t], N)][0:1, 0:rows] for t in range(noff)]
    divisors = []
    for t in range(noff):
        for s in range(npiv):
            row = norm_all[pivot_block[t, s]][0:1, :]
            pivot_norm = jnp.sum(
                jnp.where(lane == pivot_row[t, s], row, 0.0), axis=1, keepdims=True
            )
            divisors.append((own_norms * pivot_norm) * partner_norms[t])

    slots = G // 2

    def arrived(k):
        pltpu.make_async_remote_copy(
            src_ref=final.at[0, 0], dst_ref=recv.at[k],
            send_sem=send3.at[0, 0], recv_sem=recv3.at[k],
            device_id=(mate, place), device_id_type=MESH,
        ).wait_recv()

    loop(slots, arrived)
    for s in range(npiv):
        whole = recv[0, s].astype(jnp.float32)
        for k in range(1, slots):
            whole = whole + recv[k, s].astype(jnp.float32)
        for t in range(noff):
            out[t, s] = (
                whole[:, t * rows : (t + 1) * rows] / divisors[t * npiv + s]
            ).astype(out.dtype)

    for sub in range(subs):
        loop(N - 1, lambda k, sub=sub: block_copy(sub, k).wait_send())
    loop(N - 1, lambda k: norm_copy(k).wait_send())
    for g in range(groups):
        mate_copy(g).wait_send()

    for g in range(groups):
        for q in range(halves):
            @pl.when(2 * q + core != place)
            def _():
                cross_copy(g, q).wait_send()

    def sent(j):
        g, k = j // per, j % per

        @pl.when(base + index(g, k) != me)
        def _():
            final_copy(g, k).wait_send()

    @pl.when(gathers)
    def _():
        loop(G, sent)


def body(vectors, norms, offsets, pivot_block, pivot_row):
    rows, fields = vectors.shape
    N, NF = lax.axis_size("blk"), lax.axis_size("fld")
    noff, npiv = pivot_block.shape
    G = min(N, fields // LANES)
    C = fields // G
    tail = min(2, C // LANES - 1)
    widths = (C - tail * LANES,) + (LANES,) * tail
    groups = 4 if G % 4 == 0 else 1
    per = G // groups
    share = rows // NF
    halves = NF // 2
    wire = jnp.bfloat16 if share % 16 == 0 else jnp.float32
    wide = noff * rows
    slots = G // 2
    subs = len(widths)
    dims = (N, NF, G, C, widths, groups, rows, noff, npiv)
    dma = pltpu.SemaphoreType.DMA
    anywhere = pl.BlockSpec(memory_space=pl.ANY)
    return pl.pallas_call(
        functools.partial(kernel, dims),
        out_shape=jax.ShapeDtypeStruct((noff, npiv, share, rows), jnp.bfloat16),
        in_specs=[anywhere] * 5,
        out_specs=pl.BlockSpec(memory_space=pltpu.VMEM),
        scratch_shapes=[
            pltpu.SMEM(offsets.shape, jnp.int32),
            pltpu.SMEM(pivot_block.shape, jnp.int32),
            pltpu.SMEM(pivot_row.shape, jnp.int32),
            pltpu.VMEM((1, rows), jnp.bfloat16),
            dma((4,)),
            tuple(pltpu.VMEM((N, rows, width), jnp.bfloat16) for width in widths),
            pltpu.VMEM((8, LANES), jnp.float32),
            pltpu.VMEM((N, 8, LANES), jnp.float32),
            pltpu.VMEM((noff * npiv, 16, max(widths)), jnp.bfloat16),
            pltpu.VMEM((groups, per, 2, halves, npiv, share, wide), jnp.float32),
            pltpu.VMEM((groups, per, halves, npiv, share, wide), wire),
            pltpu.VMEM((groups, per, halves, npiv, share, wide), wire),
            pltpu.VMEM((groups, halves, per, npiv, share, wide), wire),
            pltpu.VMEM((groups, NF - 1, per, npiv, share, wide), wire),
            pltpu.VMEM((groups, per, npiv, share, wide), wire),
            pltpu.VMEM((slots, npiv, share, wide), wire),
            dma((subs, N)),
            dma((subs, N)),
            dma((subs,)),
            dma((N,)),
            dma((N,)),
            dma((groups,)),
            dma((groups,)),
            dma((groups, halves)),
            dma((groups, NF - 1)),
            dma((groups, per)),
            dma((slots,)),
        ],
        compiler_params=pltpu.CompilerParams(
            collective_id=0, has_side_effects=True, vmem_limit_bytes=63 * 1024 * 1024
        ),
        cost_estimate=pl.CostEstimate(
            flops=2 * noff * npiv * G * rows * rows * C,
            bytes_accessed=2 * rows * fields * 2,
            transcendentals=0,
        ),
    )(offsets, pivot_block, pivot_row, vectors, norms.reshape(1, rows))


def solution(mesh):
    return jax.shard_map(
        body,
        mesh=mesh,
        in_specs=(P("blk", "fld"), P("blk"), P(), P(), P()),
        out_specs=P(None, None, ("blk", "fld"), None),
        check_vma=False,
    )
```

```python
import functools

import jax
import jax.numpy as jnp
from jax import lax
from jax.experimental import pallas as pl
from jax.experimental.pallas import tpu as pltpu
from jax.sharding import PartitionSpec as P

MESH = pl.DeviceIdType.MESH
LANES = 128


def kernel(
    dims, offsets_in, pivot_block_in, pivot_row_in, vectors, norms_in, out,
    offsets, pivot_block, pivot_row, norms, small, gat, norm_src, norm_all, piv, acc, part, mate_in, total, cross_in, final, recv,
    send1, recv1, own1, sendn, recvn, send2, recv2, sendx, recvx, send3, recv3,
):
    N, NF, G, C, widths, groups, rows, noff, npiv = dims
    share = rows // NF
    halves = NF // 2
    subs = len(widths)
    starts = [sum(widths[:sub]) for sub in range(subs)]
    per = G // groups
    me, place = lax.axis_index("blk"), lax.axis_index("fld")
    group, chunk = me // G, me % G
    base = group * G
    core = me % 2
    mate = me + 1 - 2 * core
    slot = chunk // 2
    gathers = place % 2 == core

    barrier = pltpu.get_barrier_semaphore()

    def greet_blk(j, carry):
        pl.semaphore_signal(
            barrier, inc=1, device_id=(lax.rem(me + j, N), place), device_id_type=MESH
        )
        return carry

    def greet_fld(j, carry):
        pl.semaphore_signal(
            barrier, inc=1, device_id=(me, lax.rem(place + j, NF)), device_id_type=MESH
        )
        return carry

    lax.fori_loop(1, N, greet_blk, 0)
    lax.fori_loop(1, NF, greet_fld, 0)

    smalls = [
        pltpu.make_async_copy(src, dst, small.at[k])
        for k, (src, dst) in enumerate((
            (norms_in, norms), (offsets_in, offsets),
            (pivot_block_in, pivot_block), (pivot_row_in, pivot_row),
        ))
    ]

    def own_copy(sub):
        first = pl.multiple_of(chunk * C + starts[sub], LANES)
        return pltpu.make_async_copy(
            vectors.at[:, pl.ds(first, widths[sub])], gat[sub].at[me], own1.at[sub]
        )

    for copy in smalls:
        copy.start()
    for sub in range(subs):
        own_copy(sub).start()
    norm_src[...] = jnp.zeros_like(norm_src)
    smalls[0].wait()
    norm_src[0:1, 0:rows] = norms[...].astype(jnp.float32)
    norm_all[me] = norm_src[...]
    pl.semaphore_wait(barrier, (N - 1) + (NF - 1))

    side = N // 2

    def peer_of(k):
        half, spot = me // side, me % side
        other = k % 2 == 0
        turn = lax.rem(spot + (k + 1) // 2, side)
        return jnp.where(other, 1 - half, half) * side + turn

    def block_copy(sub, k):
        peer = peer_of(k)
        first = pl.multiple_of((peer % G) * C + starts[sub], LANES)
        return pltpu.make_async_remote_copy(
            src_ref=vectors.at[:, pl.ds(first, widths[sub])], dst_ref=gat[sub].at[me],
            send_sem=send1.at[sub], recv_sem=recv1.at[sub],
            device_id=(peer, place), device_id_type=MESH,
        )

    def norm_copy(k):
        return pltpu.make_async_remote_copy(
            src_ref=norm_src, dst_ref=norm_all.at[me],
            send_sem=sendn, recv_sem=recvn,
            device_id=(peer_of(k), place), device_id_type=MESH,
        )

    def drain(ref, sem):
        pltpu.make_async_copy(ref, ref, sem).wait()

    def loop(count, step):
        def run(k, carry):
            step(k)
            return carry

        lax.fori_loop(0, count, run, 0)

    for sub in range(subs):
        loop(N - 1, lambda k, sub=sub: block_copy(sub, k).start())
    loop(N - 1, lambda k: norm_copy(k).start())

    for copy in smalls[1:]:
        copy.wait()

    def pivots(sub):
        width = widths[sub]
        spot = lax.broadcasted_iota(jnp.int32, (rows, width), 0)
        for t in range(noff):
            for s in range(npiv):
                block = gat[sub][pivot_block[t, s]].astype(jnp.float32)
                picked = jnp.sum(
                    jnp.where(spot == pivot_row[t, s], block, 0.0), axis=0, keepdims=True
                )
                piv[t * npiv + s, :, 0:width] = jnp.broadcast_to(picked, (16, width)).astype(jnp.bfloat16)

    def index(g, k):
        return k * groups + (g + (groups // 2) * (k % 2)) % groups

    def tile(sub, g, k):
        block, width = base + index(g, k), widths[sub]
        resident = gat[sub][block].reshape(rows // 16, 16, width)
        ahead = [block + offsets[t] for t in range(noff)]
        partner = jnp.concatenate(
            [gat[sub][jnp.where(b < N, b, b - N)] for b in ahead], axis=0
        )
        scaled = jnp.concatenate(
            [
                (resident * piv[j, :, 0:width][None]).reshape(rows, width)
                for j in range(noff * npiv)
            ],
            axis=0,
        )
        met = lax.dot_general(
            scaled, partner, (((1,), (1,)), ((), ())), preferred_element_type=jnp.float32
        )
        lane = lax.broadcasted_iota(jnp.int32, (npiv * rows, noff * rows), 1)
        value = met[0 : npiv * rows]
        for t in range(1, noff):
            value = jnp.where(
                lane < t * rows, value, met[t * npiv * rows : (t + 1) * npiv * rows]
            )
        for s in range(npiv):
            for h in range(NF):
                first = s * rows + h * share
                piece = value[first : first + share]
                if sub > 0:
                    piece = piece + acc[g, k, h % 2, h // 2, s]
                acc[g, k, h % 2, h // 2, s] = piece

    def mate_copy(q):
        return pltpu.make_async_remote_copy(
            src_ref=part.at[q], dst_ref=mate_in.at[q],
            send_sem=send2.at[q], recv_sem=recv2.at[q],
            device_id=(mate, place), device_id_type=MESH,
        )

    def cross_copy(g, q):
        target = 2 * q + core
        lane = lax.rem(place - target + NF, NF) - 1
        return pltpu.make_async_remote_copy(
            src_ref=total.at[g, q], dst_ref=cross_in.at[g, lane],
            send_sem=sendx.at[g, q], recv_sem=recvx.at[g, lane],
            device_id=(me, target), device_id_type=MESH,
        )

    def cross_arrival(g, lane):
        return pltpu.make_async_remote_copy(
            src_ref=total.at[g, 0], dst_ref=cross_in.at[g, lane],
            send_sem=sendx.at[g, 0], recv_sem=recvx.at[g, lane],
            device_id=(me, lax.rem(place + 1, NF)), device_id_type=MESH,
        )

    def final_copy(g, k):
        return pltpu.make_async_remote_copy(
            src_ref=final.at[g * per + k], dst_ref=recv.at[slot],
            send_sem=send3, recv_sem=recv3,
            device_id=(base + index(g, k), place), device_id_type=MESH,
        )

    def over_fld(g):
        mate_copy(g).wait_recv()
        for q in range(halves):
            @pl.when(2 * q + core != place)
            def _():
                for k in range(per):
                    total[g, q, k] = (
                        acc[g, k, core, q] + mate_in[g, k, q].astype(jnp.float32)
                    ).astype(total.dtype)
                cross_copy(g, q).start()

    def over_blk(g):
        @pl.when(gathers)
        def _():
            for lane in range(NF - 1):
                cross_arrival(g, lane).wait_recv()
            for k in range(per):
                whole = acc[g, k, core, place // 2] + mate_in[g, k, place // 2].astype(jnp.float32)
                for lane in range(NF - 1):
                    whole = whole + cross_in[g, lane, k].astype(jnp.float32)
                final[g * per + k] = whole.astype(final.dtype)
                here = base + index(g, k) == me

                @pl.when(here)
                def _():
                    pltpu.make_async_copy(final.at[g * per + k], recv.at[slot], recv3).start()

                @pl.when(jnp.logical_not(here))
                def _():
                    final_copy(g, k).start()

    for sub in range(subs):
        own_copy(sub).wait()
        drain(gat[sub].at[pl.ds(0, N - 1)], recv1.at[sub])
        pivots(sub)
        if sub < subs - 1:
            def several(g, sub=sub):
                for k in range(per):
                    tile(sub, g, k)

            loop(groups, several)
    for g in range(groups):
        for k in range(per):
            tile(subs - 1, g, k)
        for k in range(per):
            part[g, k] = acc[g, k, 1 - core].astype(part.dtype)
        mate_copy(g).start()
        if g > 0:
            over_fld(g - 1)
        if g > 1:
            over_blk(g - 2)
    over_fld(groups - 1)
    if groups > 1:
        over_blk(groups - 2)
    over_blk(groups - 1)

    drain(norm_all.at[pl.ds(0, N - 1)], recvn)
    lane = lax.broadcasted_iota(jnp.int32, (1, LANES), 1)
    line = lax.broadcasted_iota(jnp.int32, (share, LANES), 0)
    cols = lax.broadcasted_iota(jnp.int32, (share, LANES), 1)
    own_norms = jnp.sum(
        jnp.where(cols == line + place * share, norm_src[0:1, :], 0.0), axis=1, keepdims=True
    )
    partner_norms = [norm_all[lax.rem(me + offsets[t], N)][0:1, 0:rows] for t in range(noff)]
    divisors = []
    for t in range(noff):
        for s in range(npiv):
            row = norm_all[pivot_block[t, s]][0:1, :]
            pivot_norm = jnp.sum(
                jnp.where(lane == pivot_row[t, s], row, 0.0), axis=1, keepdims=True
            )
            divisors.append((own_norms * pivot_norm) * partner_norms[t])

    slots = G // 2

    for sub in range(subs):
        drain(gat[sub].at[pl.ds(0, N - 1)], send1.at[sub])
    drain(norm_all.at[pl.ds(0, N - 1)], sendn)
    for g in range(groups):
        mate_copy(g).wait_send()
        for q in range(halves):
            @pl.when(2 * q + core != place)
            def _():
                cross_copy(g, q).wait_send()

    drain(recv, recv3)
    for s in range(npiv):
        whole = recv[0, s].astype(jnp.float32)
        for k in range(1, slots):
            whole = whole + recv[k, s].astype(jnp.float32)
        for t in range(noff):
            out[t, s] = (
                whole[:, t * rows : (t + 1) * rows] / divisors[t * npiv + s]
            ).astype(out.dtype)

    @pl.when(gathers)
    def _():
        drain(final.at[pl.ds(0, G - 1)], send3)


def body(vectors, norms, offsets, pivot_block, pivot_row):
    rows, fields = vectors.shape
    N, NF = lax.axis_size("blk"), lax.axis_size("fld")
    noff, npiv = pivot_block.shape
    G = min(N, fields // LANES)
    C = fields // G
    widths = (C // 2, C // 2) if C % (2 * LANES) == 0 else (C,)
    groups = 4 if G % 4 == 0 else 1
    per = G // groups
    share = rows // NF
    halves = NF // 2
    wire = jnp.bfloat16 if share % 16 == 0 else jnp.float32
    wide = noff * rows
    slots = G // 2
    subs = len(widths)
    dims = (N, NF, G, C, widths, groups, rows, noff, npiv)
    dma = pltpu.SemaphoreType.DMA
    anywhere = pl.BlockSpec(memory_space=pl.ANY)
    return pl.pallas_call(
        functools.partial(kernel, dims),
        out_shape=jax.ShapeDtypeStruct((noff, npiv, share, rows), jnp.bfloat16),
        in_specs=[anywhere] * 5,
        out_specs=pl.BlockSpec(memory_space=pltpu.VMEM),
        scratch_shapes=[
            pltpu.SMEM(offsets.shape, jnp.int32),
            pltpu.SMEM(pivot_block.shape, jnp.int32),
            pltpu.SMEM(pivot_row.shape, jnp.int32),
            pltpu.VMEM((1, rows), jnp.bfloat16),
            dma((4,)),
            tuple(pltpu.VMEM((N, rows, width), jnp.bfloat16) for width in widths),
            pltpu.VMEM((8, LANES), jnp.float32),
            pltpu.VMEM((N, 8, LANES), jnp.float32),
            pltpu.VMEM((noff * npiv, 16, max(widths)), jnp.bfloat16),
            pltpu.VMEM((groups, per, 2, halves, npiv, share, wide), jnp.float32),
            pltpu.VMEM((groups, per, halves, npiv, share, wide), wire),
            pltpu.VMEM((groups, per, halves, npiv, share, wide), wire),
            pltpu.VMEM((groups, halves, per, npiv, share, wide), wire),
            pltpu.VMEM((groups, NF - 1, per, npiv, share, wide), wire),
            pltpu.VMEM((G, npiv, share, wide), wire),
            pltpu.VMEM((slots, npiv, share, wide), wire),
            dma((subs,)),
            dma((subs,)),
            dma((subs,)),
            dma,
            dma,
            dma((groups,)),
            dma((groups,)),
            dma((groups, halves)),
            dma((groups, NF - 1)),
            dma,
            dma,
        ],
        compiler_params=pltpu.CompilerParams(
            collective_id=0, has_side_effects=True, vmem_limit_bytes=63 * 1024 * 1024
        ),
        cost_estimate=pl.CostEstimate(
            flops=2 * noff * npiv * G * rows * rows * C,
            bytes_accessed=2 * rows * fields * 2,
            transcendentals=0,
        ),
    )(offsets, pivot_block, pivot_row, vectors, norms.reshape(1, rows))


def solution(mesh):
    return jax.shard_map(
        body,
        mesh=mesh,
        in_specs=(P("blk", "fld"), P("blk"), P(), P(), P()),
        out_specs=P(None, None, ("blk", "fld"), None),
        check_vma=False,
    )
```

```python
import functools

import jax
import jax.numpy as jnp
from jax import lax
from jax.experimental import pallas as pl
from jax.experimental.pallas import tpu as pltpu
from jax.sharding import PartitionSpec as P

MESH = pl.DeviceIdType.MESH
LANES = 128


def kernel(
    dims, offsets_in, pivot_block_in, pivot_row_in, vectors, norms_in, out,
    offsets, pivot_block, pivot_row, norms, small, gat, norm_src, norm_all, piv, acc, part, mate_in, total, cross_in, final, recv,
    send1, recv1, own1, sendn, recvn, send2, recv2, sendx, recvx, send3, recv3,
):
    N, NF, G, C, widths, groups, rows, noff, npiv = dims
    share = rows // NF
    halves = NF // 2
    subs = len(widths)
    starts = [sum(widths[:sub]) for sub in range(subs)]
    per = G // groups
    me, place = lax.axis_index("blk"), lax.axis_index("fld")
    group, chunk = me // G, me % G
    base = group * G
    core = me % 2
    mate = me + 1 - 2 * core
    slot = chunk // 2
    gathers = place % 2 == core

    barrier = pltpu.get_barrier_semaphore()

    def greet_blk(j, carry):
        pl.semaphore_signal(
            barrier, inc=1, device_id=(lax.rem(me + j, N), place), device_id_type=MESH
        )
        return carry

    def greet_fld(j, carry):
        pl.semaphore_signal(
            barrier, inc=1, device_id=(me, lax.rem(place + j, NF)), device_id_type=MESH
        )
        return carry

    lax.fori_loop(1, N, greet_blk, 0)
    lax.fori_loop(1, NF, greet_fld, 0)

    smalls = [
        pltpu.make_async_copy(src, dst, small.at[k])
        for k, (src, dst) in enumerate((
            (norms_in, norms), (offsets_in, offsets),
            (pivot_block_in, pivot_block), (pivot_row_in, pivot_row),
        ))
    ]

    def own_copy(sub):
        first = pl.multiple_of(chunk * C + starts[sub], LANES)
        return pltpu.make_async_copy(
            vectors.at[:, pl.ds(first, widths[sub])], gat[sub].at[me], own1.at[sub]
        )

    for copy in smalls:
        copy.start()
    for sub in range(subs):
        own_copy(sub).start()
    norm_src[...] = jnp.zeros_like(norm_src)
    smalls[0].wait()
    norm_src[0:1, 0:rows] = norms[...].astype(jnp.float32)
    norm_all[me] = norm_src[...]
    pl.semaphore_wait(barrier, (N - 1) + (NF - 1))

    side = N // 2

    def peer_of(k):
        half, spot = me // side, me % side
        other = k % 2 == 0
        turn = lax.rem(spot + (k + 1) // 2, side)
        return jnp.where(other, 1 - half, half) * side + turn

    def block_copy(sub, k):
        peer = peer_of(k)
        first = pl.multiple_of((peer % G) * C + starts[sub], LANES)
        return pltpu.make_async_remote_copy(
            src_ref=vectors.at[:, pl.ds(first, widths[sub])], dst_ref=gat[sub].at[me],
            send_sem=send1.at[sub], recv_sem=recv1.at[sub],
            device_id=(peer, place), device_id_type=MESH,
        )

    def norm_copy(k):
        return pltpu.make_async_remote_copy(
            src_ref=norm_src, dst_ref=norm_all.at[me],
            send_sem=sendn, recv_sem=recvn,
            device_id=(peer_of(k), place), device_id_type=MESH,
        )

    def drain(ref, sem):
        pltpu.make_async_copy(ref, ref, sem).wait()

    def loop(count, step):
        def run(k, carry):
            step(k)
            return carry

        lax.fori_loop(0, count, run, 0)

    for sub in range(subs):
        loop(N - 1, lambda k, sub=sub: block_copy(sub, k).start())
    loop(N - 1, lambda k: norm_copy(k).start())

    for copy in smalls[1:]:
        copy.wait()

    def pivots(sub):
        width = widths[sub]
        spot = lax.broadcasted_iota(jnp.int32, (rows, width), 0)
        for t in range(noff):
            for s in range(npiv):
                block = gat[sub][pivot_block[t, s]].astype(jnp.float32)
                picked = jnp.sum(
                    jnp.where(spot == pivot_row[t, s], block, 0.0), axis=0, keepdims=True
                )
                piv[t * npiv + s, :, 0:width] = jnp.broadcast_to(picked, (16, width)).astype(jnp.bfloat16)

    def index(g, k):
        return k * groups + (g + (groups // 2) * (k % 2)) % groups

    def tile(sub, g, k):
        block, width = base + index(g, k), widths[sub]
        resident = gat[sub][block].reshape(rows // 16, 16, width)
        ahead = [block + offsets[t] for t in range(noff)]
        partner = jnp.concatenate(
            [gat[sub][jnp.where(b < N, b, b - N)] for b in ahead], axis=0
        )
        scaled = jnp.concatenate(
            [
                (resident * piv[j, :, 0:width][None]).reshape(rows, width)
                for j in range(noff * npiv)
            ],
            axis=0,
        )
        met = lax.dot_general(
            scaled, partner, (((1,), (1,)), ((), ())), preferred_element_type=jnp.float32
        )
        lane = lax.broadcasted_iota(jnp.int32, (npiv * rows, noff * rows), 1)
        value = met[0 : npiv * rows]
        for t in range(1, noff):
            value = jnp.where(
                lane < t * rows, value, met[t * npiv * rows : (t + 1) * npiv * rows]
            )
        pieces = {}
        for s in range(npiv):
            for h in range(NF):
                first = s * rows + h * share
                pieces[h % 2, h // 2, s] = value[first : first + share]
                if sub > 0:
                    pieces[h % 2, h // 2, s] += acc[g, k, h % 2, h // 2, s]
        return pieces

    def tiles(sub, g):
        for first in range(0, per, 2):
            pair = range(first, min(first + 2, per))
            found = [tile(sub, g, k) for k in pair]
            for k, pieces in zip(pair, found):
                for (c, q, s), piece in pieces.items():
                    acc[g, k, c, q, s] = piece

    def mate_copy(q):
        return pltpu.make_async_remote_copy(
            src_ref=part.at[q], dst_ref=mate_in.at[q],
            send_sem=send2.at[q], recv_sem=recv2.at[q],
            device_id=(mate, place), device_id_type=MESH,
        )

    def cross_copy(g, q):
        target = 2 * q + core
        lane = lax.rem(place - target + NF, NF) - 1
        return pltpu.make_async_remote_copy(
            src_ref=total.at[g, q], dst_ref=cross_in.at[g, lane],
            send_sem=sendx.at[g, q], recv_sem=recvx.at[g, lane],
            device_id=(me, target), device_id_type=MESH,
        )

    def cross_arrival(g, lane):
        return pltpu.make_async_remote_copy(
            src_ref=total.at[g, 0], dst_ref=cross_in.at[g, lane],
            send_sem=sendx.at[g, 0], recv_sem=recvx.at[g, lane],
            device_id=(me, lax.rem(place + 1, NF)), device_id_type=MESH,
        )

    def final_copy(g, k):
        return pltpu.make_async_remote_copy(
            src_ref=final.at[g * per + k], dst_ref=recv.at[slot],
            send_sem=send3, recv_sem=recv3,
            device_id=(base + index(g, k), place), device_id_type=MESH,
        )

    def over_fld(g):
        mate_copy(g).wait_recv()
        for q in range(halves):
            @pl.when(2 * q + core != place)
            def _():
                for k in range(per):
                    total[g, q, k] = (
                        acc[g, k, core, q] + mate_in[g, k, q].astype(jnp.float32)
                    ).astype(total.dtype)
                cross_copy(g, q).start()

    def over_blk(g):
        @pl.when(gathers)
        def _():
            for lane in range(NF - 1):
                cross_arrival(g, lane).wait_recv()
            for k in range(per):
                whole = acc[g, k, core, place // 2] + mate_in[g, k, place // 2].astype(jnp.float32)
                for lane in range(NF - 1):
                    whole = whole + cross_in[g, lane, k].astype(jnp.float32)
                final[g * per + k] = whole.astype(final.dtype)
                here = base + index(g, k) == me

                @pl.when(here)
                def _():
                    pltpu.make_async_copy(final.at[g * per + k], recv.at[slot], recv3).start()

                @pl.when(jnp.logical_not(here))
                def _():
                    final_copy(g, k).start()

    for sub in range(subs):
        own_copy(sub).wait()
        drain(gat[sub].at[pl.ds(0, N - 1)], recv1.at[sub])
        pivots(sub)
        if sub < subs - 1:
            def several(g, sub=sub):
                tiles(sub, g)

            loop(groups, several)
    for g in range(groups):
        tiles(subs - 1, g)
        for k in range(per):
            part[g, k] = acc[g, k, 1 - core].astype(part.dtype)
        mate_copy(g).start()
        if g > 0:
            over_fld(g - 1)
        if g > 1:
            over_blk(g - 2)
    over_fld(groups - 1)
    if groups > 1:
        over_blk(groups - 2)
    over_blk(groups - 1)

    drain(norm_all.at[pl.ds(0, N - 1)], recvn)
    lane = lax.broadcasted_iota(jnp.int32, (1, LANES), 1)
    line = lax.broadcasted_iota(jnp.int32, (share, LANES), 0)
    cols = lax.broadcasted_iota(jnp.int32, (share, LANES), 1)
    own_norms = jnp.sum(
        jnp.where(cols == line + place * share, norm_src[0:1, :], 0.0), axis=1, keepdims=True
    )
    partner_norms = [norm_all[lax.rem(me + offsets[t], N)][0:1, 0:rows] for t in range(noff)]
    divisors = []
    for t in range(noff):
        for s in range(npiv):
            row = norm_all[pivot_block[t, s]][0:1, :]
            pivot_norm = jnp.sum(
                jnp.where(lane == pivot_row[t, s], row, 0.0), axis=1, keepdims=True
            )
            divisors.append((own_norms * pivot_norm) * partner_norms[t])

    slots = G // 2

    for sub in range(subs):
        drain(gat[sub].at[pl.ds(0, N - 1)], send1.at[sub])
    drain(norm_all.at[pl.ds(0, N - 1)], sendn)
    for g in range(groups):
        mate_copy(g).wait_send()
        for q in range(halves):
            @pl.when(2 * q + core != place)
            def _():
                cross_copy(g, q).wait_send()

    drain(recv, recv3)
    for s in range(npiv):
        whole = recv[0, s].astype(jnp.float32)
        for k in range(1, slots):
            whole = whole + recv[k, s].astype(jnp.float32)
        for t in range(noff):
            out[t, s] = (
                whole[:, t * rows : (t + 1) * rows] / divisors[t * npiv + s]
            ).astype(out.dtype)

    @pl.when(gathers)
    def _():
        drain(final.at[pl.ds(0, G - 1)], send3)


def body(vectors, norms, offsets, pivot_block, pivot_row):
    rows, fields = vectors.shape
    N, NF = lax.axis_size("blk"), lax.axis_size("fld")
    noff, npiv = pivot_block.shape
    G = min(N, fields // LANES)
    C = fields // G
    widths = (C // 2, C // 2) if C % (2 * LANES) == 0 else (C,)
    groups = 4 if G % 4 == 0 else 1
    per = G // groups
    share = rows // NF
    halves = NF // 2
    wire = jnp.bfloat16 if share % 16 == 0 else jnp.float32
    wide = noff * rows
    slots = G // 2
    subs = len(widths)
    dims = (N, NF, G, C, widths, groups, rows, noff, npiv)
    dma = pltpu.SemaphoreType.DMA
    anywhere = pl.BlockSpec(memory_space=pl.ANY)
    return pl.pallas_call(
        functools.partial(kernel, dims),
        out_shape=jax.ShapeDtypeStruct((noff, npiv, share, rows), jnp.bfloat16),
        in_specs=[anywhere] * 5,
        out_specs=pl.BlockSpec(memory_space=pltpu.VMEM),
        scratch_shapes=[
            pltpu.SMEM(offsets.shape, jnp.int32),
            pltpu.SMEM(pivot_block.shape, jnp.int32),
            pltpu.SMEM(pivot_row.shape, jnp.int32),
            pltpu.VMEM((1, rows), jnp.bfloat16),
            dma((4,)),
            tuple(pltpu.VMEM((N, rows, width), jnp.bfloat16) for width in widths),
            pltpu.VMEM((8, LANES), jnp.float32),
            pltpu.VMEM((N, 8, LANES), jnp.float32),
            pltpu.VMEM((noff * npiv, 16, max(widths)), jnp.bfloat16),
            pltpu.VMEM((groups, per, 2, halves, npiv, share, wide), jnp.float32),
            pltpu.VMEM((groups, per, halves, npiv, share, wide), wire),
            pltpu.VMEM((groups, per, halves, npiv, share, wide), wire),
            pltpu.VMEM((groups, halves, per, npiv, share, wide), wire),
            pltpu.VMEM((groups, NF - 1, per, npiv, share, wide), wire),
            pltpu.VMEM((G, npiv, share, wide), wire),
            pltpu.VMEM((slots, npiv, share, wide), wire),
            dma((subs,)),
            dma((subs,)),
            dma((subs,)),
            dma,
            dma,
            dma((groups,)),
            dma((groups,)),
            dma((groups, halves)),
            dma((groups, NF - 1)),
            dma,
            dma,
        ],
        compiler_params=pltpu.CompilerParams(
            collective_id=0, has_side_effects=True, vmem_limit_bytes=63 * 1024 * 1024
        ),
        cost_estimate=pl.CostEstimate(
            flops=2 * noff * npiv * G * rows * rows * C,
            bytes_accessed=2 * rows * fields * 2,
            transcendentals=0,
        ),
    )(offsets, pivot_block, pivot_row, vectors, norms.reshape(1, rows))


def solution(mesh):
    return jax.shard_map(
        body,
        mesh=mesh,
        in_specs=(P("blk", "fld"), P("blk"), P(), P(), P()),
        out_specs=P(None, None, ("blk", "fld"), None),
        check_vma=False,
    )
```

```python
import functools

import jax
import jax.numpy as jnp
from jax import lax
from jax.experimental import pallas as pl
from jax.experimental.pallas import tpu as pltpu
from jax.sharding import PartitionSpec as P

MESH = pl.DeviceIdType.MESH
LANES = 128


def kernel(
    dims, offsets_in, pivot_block_in, pivot_row_in, vectors, norms_in, out,
    offsets, pivot_block, pivot_row, norms, small, gat, norm_src, norm_all, piv, acc, part, mate_in, total, cross_in, final, recv,
    send1, recv1, own1, sendn, recvn, send2, recv2, sendx, recvx, send3, recv3,
):
    N, NF, G, C, widths, groups, rows, noff, npiv = dims
    share = rows // NF
    halves = NF // 2
    subs = len(widths)
    starts = [sum(widths[:sub]) for sub in range(subs)]
    per = G // groups
    me, place = lax.axis_index("blk"), lax.axis_index("fld")
    group, chunk = me // G, me % G
    base = group * G
    core = me % 2
    mate = me + 1 - 2 * core
    slot = chunk // 2
    gathers = place % 2 == core

    barrier = pltpu.get_barrier_semaphore()

    def greet_blk(j, carry):
        pl.semaphore_signal(
            barrier, inc=1, device_id=(lax.rem(me + j, N), place), device_id_type=MESH
        )
        return carry

    def greet_fld(j, carry):
        pl.semaphore_signal(
            barrier, inc=1, device_id=(me, lax.rem(place + j, NF)), device_id_type=MESH
        )
        return carry

    lax.fori_loop(1, N, greet_blk, 0)
    lax.fori_loop(1, NF, greet_fld, 0)

    smalls = [
        pltpu.make_async_copy(src, dst, small.at[k])
        for k, (src, dst) in enumerate((
            (norms_in, norms), (offsets_in, offsets),
            (pivot_block_in, pivot_block), (pivot_row_in, pivot_row),
        ))
    ]

    def own_copy(sub):
        first = pl.multiple_of(chunk * C + starts[sub], LANES)
        return pltpu.make_async_copy(
            vectors.at[:, pl.ds(first, widths[sub])], gat[sub].at[me], own1.at[sub]
        )

    for copy in smalls:
        copy.start()
    for sub in range(subs):
        own_copy(sub).start()
    norm_src[...] = jnp.zeros_like(norm_src)
    smalls[0].wait()
    norm_src[0:1, 0:rows] = norms[...].astype(jnp.float32)
    norm_all[me] = norm_src[...]
    pl.semaphore_wait(barrier, (N - 1) + (NF - 1))

    side = N // 2

    def peer_of(k):
        half, spot = me // side, me % side
        other = k % 2 == 0
        turn = lax.rem(spot + (k + 1) // 2, side)
        return jnp.where(other, 1 - half, half) * side + turn

    def block_copy(sub, k):
        peer = peer_of(k)
        first = pl.multiple_of((peer % G) * C + starts[sub], LANES)
        return pltpu.make_async_remote_copy(
            src_ref=vectors.at[:, pl.ds(first, widths[sub])], dst_ref=gat[sub].at[me],
            send_sem=send1.at[sub], recv_sem=recv1.at[sub],
            device_id=(peer, place), device_id_type=MESH,
        )

    def norm_copy(k):
        return pltpu.make_async_remote_copy(
            src_ref=norm_src, dst_ref=norm_all.at[me],
            send_sem=sendn, recv_sem=recvn,
            device_id=(peer_of(k), place), device_id_type=MESH,
        )

    def drain(ref, sem):
        pltpu.make_async_copy(ref, ref, sem).wait()

    def loop(count, step):
        def run(k, carry):
            step(k)
            return carry

        lax.fori_loop(0, count, run, 0)

    for sub in range(subs):
        loop(N - 1, lambda k, sub=sub: block_copy(sub, k).start())
    loop(N - 1, lambda k: norm_copy(k).start())

    for copy in smalls[1:]:
        copy.wait()

    def pivots(sub):
        width = widths[sub]
        spot = lax.broadcasted_iota(jnp.int32, (rows, width), 0)
        for t in range(noff):
            for s in range(npiv):
                block = gat[sub][pivot_block[t, s]].astype(jnp.float32)
                picked = jnp.sum(
                    jnp.where(spot == pivot_row[t, s], block, 0.0), axis=0, keepdims=True
                )
                piv[t * npiv + s, :, 0:width] = jnp.broadcast_to(picked, (16, width)).astype(jnp.bfloat16)

    def index(g, k):
        return k * groups + (g + (groups // 2) * (k % 2)) % groups

    def tile(sub, g, k):
        block, width = base + index(g, k), widths[sub]
        resident = gat[sub][block].reshape(rows // 16, 16, width)
        ahead = [block + offsets[t] for t in range(noff)]
        partner = jnp.concatenate(
            [gat[sub][jnp.where(b < N, b, b - N)] for b in ahead], axis=0
        )
        scaled = jnp.concatenate(
            [
                (resident * piv[j, :, 0:width][None]).reshape(rows, width)
                for j in range(noff * npiv)
            ],
            axis=0,
        )
        met = lax.dot_general(
            scaled, partner, (((1,), (1,)), ((), ())), preferred_element_type=jnp.float32
        )
        lane = lax.broadcasted_iota(jnp.int32, (npiv * rows, noff * rows), 1)
        value = met[0 : npiv * rows]
        for t in range(1, noff):
            value = jnp.where(
                lane < t * rows, value, met[t * npiv * rows : (t + 1) * npiv * rows]
            )
        pieces = {}
        for s in range(npiv):
            for h in range(NF):
                first = s * rows + h * share
                pieces[h % 2, h // 2, s] = value[first : first + share]
                if sub > 0:
                    pieces[h % 2, h // 2, s] += acc[g, k, h % 2, h // 2, s]
        return pieces

    def tiles(sub, g):
        for first in range(0, per, 2):
            pair = range(first, min(first + 2, per))
            found = [tile(sub, g, k) for k in pair]
            for k, pieces in zip(pair, found):
                for (c, q, s), piece in pieces.items():
                    acc[g, k, c, q, s] = piece

    def mate_copy(q):
        return pltpu.make_async_remote_copy(
            src_ref=part.at[q], dst_ref=mate_in.at[q],
            send_sem=send2.at[q], recv_sem=recv2.at[q],
            device_id=(mate, place), device_id_type=MESH,
        )

    def cross_copy(g, q):
        target = 2 * q + core
        lane = lax.rem(place - target + NF, NF) - 1
        return pltpu.make_async_remote_copy(
            src_ref=total.at[g, q], dst_ref=cross_in.at[g, lane],
            send_sem=sendx.at[g, q], recv_sem=recvx.at[g, lane],
            device_id=(me, target), device_id_type=MESH,
        )

    def cross_arrival(g, lane):
        return pltpu.make_async_remote_copy(
            src_ref=total.at[g, 0], dst_ref=cross_in.at[g, lane],
            send_sem=sendx.at[g, 0], recv_sem=recvx.at[g, lane],
            device_id=(me, lax.rem(place + 1, NF)), device_id_type=MESH,
        )

    def final_copy(g, k):
        return pltpu.make_async_remote_copy(
            src_ref=final.at[g * per + k], dst_ref=recv.at[slot],
            send_sem=send3, recv_sem=recv3,
            device_id=(base + index(g, k), place), device_id_type=MESH,
        )

    def over_fld(g):
        mate_copy(g).wait_recv()
        for q in range(halves):
            @pl.when(2 * q + core != place)
            def _():
                for k in range(per):
                    total[g, q, k] = (
                        acc[g, k, core, q] + mate_in[g, k, q].astype(jnp.float32)
                    ).astype(total.dtype)
                cross_copy(g, q).start()

    def over_blk(g):
        @pl.when(gathers)
        def _():
            for lane in range(NF - 1):
                cross_arrival(g, lane).wait_recv()
            for k in range(per):
                whole = acc[g, k, core, place // 2] + mate_in[g, k, place // 2].astype(jnp.float32)
                for lane in range(NF - 1):
                    whole = whole + cross_in[g, lane, k].astype(jnp.float32)
                final[g * per + k] = whole.astype(final.dtype)
                here = base + index(g, k) == me

                @pl.when(here)
                def _():
                    pltpu.make_async_copy(final.at[g * per + k], recv.at[slot], recv3).start()

                @pl.when(jnp.logical_not(here))
                def _():
                    final_copy(g, k).start()

    for sub in range(subs):
        own_copy(sub).wait()
        drain(gat[sub].at[pl.ds(0, N - 1)], recv1.at[sub])
        pivots(sub)
        if sub < subs - 1:
            def several(g, sub=sub):
                tiles(sub, g)

            loop(groups, several)
    for g in range(groups):
        tiles(subs - 1, g)
        for k in range(per):
            part[g, k] = acc[g, k, 1 - core].astype(part.dtype)
        mate_copy(g).start()
        if g > 0:
            over_fld(g - 1)
        if g > 1:
            over_blk(g - 2)
    over_fld(groups - 1)
    if groups > 1:
        over_blk(groups - 2)
    over_blk(groups - 1)

    drain(norm_all.at[pl.ds(0, N - 1)], recvn)
    lane = lax.broadcasted_iota(jnp.int32, (1, LANES), 1)
    line = lax.broadcasted_iota(jnp.int32, (share, LANES), 0)
    cols = lax.broadcasted_iota(jnp.int32, (share, LANES), 1)
    own_norms = jnp.sum(
        jnp.where(cols == line + place * share, norm_src[0:1, :], 0.0), axis=1, keepdims=True
    )
    partner_norms = [norm_all[lax.rem(me + offsets[t], N)][0:1, 0:rows] for t in range(noff)]
    divisors = []
    for t in range(noff):
        for s in range(npiv):
            row = norm_all[pivot_block[t, s]][0:1, :]
            pivot_norm = jnp.sum(
                jnp.where(lane == pivot_row[t, s], row, 0.0), axis=1, keepdims=True
            )
            divisors.append((own_norms * pivot_norm) * partner_norms[t])

    slots = G // 2

    for sub in range(subs):
        drain(gat[sub].at[pl.ds(0, N - 1)], send1.at[sub])
    drain(norm_all.at[pl.ds(0, N - 1)], sendn)
    for g in range(groups):
        mate_copy(g).wait_send()
        for q in range(halves):
            @pl.when(2 * q + core != place)
            def _():
                cross_copy(g, q).wait_send()

    drain(recv, recv3)
    for s in range(npiv):
        whole = recv[0, s].astype(jnp.float32)
        for k in range(1, slots):
            whole = whole + recv[k, s].astype(jnp.float32)
        for t in range(noff):
            out[t, s] = (
                whole[:, t * rows : (t + 1) * rows] / divisors[t * npiv + s]
            ).astype(out.dtype)

    @pl.when(gathers)
    def _():
        drain(final.at[pl.ds(0, G - 1)], send3)


def body(vectors, norms, offsets, pivot_block, pivot_row):
    rows, fields = vectors.shape
    N, NF = lax.axis_size("blk"), lax.axis_size("fld")
    noff, npiv = pivot_block.shape
    G = min(N, fields // LANES)
    C = fields // G
    widths = (C,)
    groups = 4 if G % 4 == 0 else 1
    per = G // groups
    share = rows // NF
    halves = NF // 2
    wire = jnp.bfloat16 if share % 16 == 0 else jnp.float32
    wide = noff * rows
    slots = G // 2
    subs = len(widths)
    dims = (N, NF, G, C, widths, groups, rows, noff, npiv)
    dma = pltpu.SemaphoreType.DMA
    anywhere = pl.BlockSpec(memory_space=pl.ANY)
    return pl.pallas_call(
        functools.partial(kernel, dims),
        out_shape=jax.ShapeDtypeStruct((noff, npiv, share, rows), jnp.bfloat16),
        in_specs=[anywhere] * 5,
        out_specs=pl.BlockSpec(memory_space=pltpu.VMEM),
        scratch_shapes=[
            pltpu.SMEM(offsets.shape, jnp.int32),
            pltpu.SMEM(pivot_block.shape, jnp.int32),
            pltpu.SMEM(pivot_row.shape, jnp.int32),
            pltpu.VMEM((1, rows), jnp.bfloat16),
            dma((4,)),
            tuple(pltpu.VMEM((N, rows, width), jnp.bfloat16) for width in widths),
            pltpu.VMEM((8, LANES), jnp.float32),
            pltpu.VMEM((N, 8, LANES), jnp.float32),
            pltpu.VMEM((noff * npiv, 16, max(widths)), jnp.bfloat16),
            pltpu.VMEM((groups, per, 2, halves, npiv, share, wide), jnp.float32),
            pltpu.VMEM((groups, per, halves, npiv, share, wide), wire),
            pltpu.VMEM((groups, per, halves, npiv, share, wide), wire),
            pltpu.VMEM((groups, halves, per, npiv, share, wide), wire),
            pltpu.VMEM((groups, NF - 1, per, npiv, share, wide), wire),
            pltpu.VMEM((G, npiv, share, wide), wire),
            pltpu.VMEM((slots, npiv, share, wide), wire),
            dma((subs,)),
            dma((subs,)),
            dma((subs,)),
            dma,
            dma,
            dma((groups,)),
            dma((groups,)),
            dma((groups, halves)),
            dma((groups, NF - 1)),
            dma,
            dma,
        ],
        compiler_params=pltpu.CompilerParams(
            collective_id=0, has_side_effects=True, vmem_limit_bytes=63 * 1024 * 1024
        ),
        cost_estimate=pl.CostEstimate(
            flops=2 * noff * npiv * G * rows * rows * C,
            bytes_accessed=2 * rows * fields * 2,
            transcendentals=0,
        ),
    )(offsets, pivot_block, pivot_row, vectors, norms.reshape(1, rows))


def solution(mesh):
    return jax.shard_map(
        body,
        mesh=mesh,
        in_specs=(P("blk", "fld"), P("blk"), P(), P(), P()),
        out_specs=P(None, None, ("blk", "fld"), None),
        check_vma=False,
    )
```

```python
import functools

import jax
import jax.numpy as jnp
from jax import lax
from jax.experimental import pallas as pl
from jax.experimental.pallas import tpu as pltpu
from jax.sharding import PartitionSpec as P

MESH = pl.DeviceIdType.MESH
LANES = 128


def kernel(
    dims, offsets_in, pivot_block_in, pivot_row_in, vectors, norms_in, out,
    offsets, pivot_block, pivot_row, norms, small, gat, norm_src, norm_all, piv, acc, part, mate_in, total, recv,
    send1, recv1, own1, sendn, recvn, send2, recv2, send3, recv3,
):
    N, NF, G, C, widths, groups, rows, noff, npiv = dims
    share = rows // NF
    halves = NF // 2
    subs = len(widths)
    starts = [sum(widths[:sub]) for sub in range(subs)]
    per = G // groups
    me, place = lax.axis_index("blk"), lax.axis_index("fld")
    group, chunk = me // G, me % G
    base = group * G
    core = me % 2
    mate = me + 1 - 2 * core
    slot = (chunk // 2) * NF + place
    gathers = place % 2 == core

    barrier = pltpu.get_barrier_semaphore()

    def greet_blk(j, carry):
        pl.semaphore_signal(
            barrier, inc=1, device_id=(lax.rem(me + j, N), place), device_id_type=MESH
        )
        return carry

    def greet_fld(j, carry):
        other = lax.rem(place + 1 + j // G, NF)
        pl.semaphore_signal(
            barrier, inc=1, device_id=(base + j % G, other), device_id_type=MESH
        )
        return carry

    lax.fori_loop(1, N, greet_blk, 0)
    lax.fori_loop(0, G * (NF - 1), greet_fld, 0)

    smalls = [
        pltpu.make_async_copy(src, dst, small.at[k])
        for k, (src, dst) in enumerate((
            (norms_in, norms), (offsets_in, offsets),
            (pivot_block_in, pivot_block), (pivot_row_in, pivot_row),
        ))
    ]

    def own_copy(sub):
        first = pl.multiple_of(chunk * C + starts[sub], LANES)
        return pltpu.make_async_copy(
            vectors.at[:, pl.ds(first, widths[sub])], gat[sub].at[me], own1.at[sub]
        )

    for copy in smalls:
        copy.start()
    for sub in range(subs):
        own_copy(sub).start()
    norm_src[...] = jnp.zeros_like(norm_src)
    smalls[0].wait()
    norm_src[0:1, 0:rows] = norms[...].astype(jnp.float32)
    norm_all[me] = norm_src[...]
    pl.semaphore_wait(barrier, (N - 1) + G * (NF - 1))

    side = N // 2

    def peer_of(k):
        half, spot = me // side, me % side
        other = k % 2 == 0
        turn = lax.rem(spot + (k + 1) // 2, side)
        return jnp.where(other, 1 - half, half) * side + turn

    def block_copy(sub, k):
        peer = peer_of(k)
        first = pl.multiple_of((peer % G) * C + starts[sub], LANES)
        return pltpu.make_async_remote_copy(
            src_ref=vectors.at[:, pl.ds(first, widths[sub])], dst_ref=gat[sub].at[me],
            send_sem=send1.at[sub], recv_sem=recv1.at[sub],
            device_id=(peer, place), device_id_type=MESH,
        )

    def norm_copy(k):
        return pltpu.make_async_remote_copy(
            src_ref=norm_src, dst_ref=norm_all.at[me],
            send_sem=sendn, recv_sem=recvn,
            device_id=(peer_of(k), place), device_id_type=MESH,
        )

    def drain(ref, sem):
        pltpu.make_async_copy(ref, ref, sem).wait()

    def loop(count, step):
        def run(k, carry):
            step(k)
            return carry

        lax.fori_loop(0, count, run, 0)

    for sub in range(subs):
        loop(N - 1, lambda k, sub=sub: block_copy(sub, k).start())
    loop(N - 1, lambda k: norm_copy(k).start())

    for copy in smalls[1:]:
        copy.wait()

    def pivots(sub):
        width = widths[sub]
        spot = lax.broadcasted_iota(jnp.int32, (rows, width), 0)
        for t in range(noff):
            for s in range(npiv):
                block = gat[sub][pivot_block[t, s]].astype(jnp.float32)
                picked = jnp.sum(
                    jnp.where(spot == pivot_row[t, s], block, 0.0), axis=0, keepdims=True
                )
                piv[t * npiv + s, :, 0:width] = jnp.broadcast_to(picked, (16, width)).astype(jnp.bfloat16)

    def index(g, k):
        return k * groups + (g + (groups // 2) * (k % 2)) % groups

    def tile(sub, g, k):
        block, width = base + index(g, k), widths[sub]
        resident = gat[sub][block].reshape(rows // 16, 16, width)
        ahead = [block + offsets[t] for t in range(noff)]
        partner = jnp.concatenate(
            [gat[sub][jnp.where(b < N, b, b - N)] for b in ahead], axis=0
        )
        scaled = jnp.concatenate(
            [
                (resident * piv[j, :, 0:width][None]).reshape(rows, width)
                for j in range(noff * npiv)
            ],
            axis=0,
        )
        met = lax.dot_general(
            scaled, partner, (((1,), (1,)), ((), ())), preferred_element_type=jnp.float32
        )
        lane = lax.broadcasted_iota(jnp.int32, (npiv * rows, noff * rows), 1)
        value = met[0 : npiv * rows]
        for t in range(1, noff):
            value = jnp.where(
                lane < t * rows, value, met[t * npiv * rows : (t + 1) * npiv * rows]
            )
        pieces = {}
        for s in range(npiv):
            for h in range(NF):
                first = s * rows + h * share
                pieces[h % 2, h // 2, s] = value[first : first + share]
                if sub > 0:
                    pieces[h % 2, h // 2, s] += acc[g, k, h % 2, h // 2, s]
        return pieces

    def tiles(sub, g):
        for first in range(0, per, 2):
            pair = range(first, min(first + 2, per))
            found = [tile(sub, g, k) for k in pair]
            for k, pieces in zip(pair, found):
                for (c, q, s), piece in pieces.items():
                    acc[g, k, c, q, s] = piece

    def mate_copy(q):
        return pltpu.make_async_remote_copy(
            src_ref=part.at[q], dst_ref=mate_in.at[q],
            send_sem=send2.at[q], recv_sem=recv2.at[q],
            device_id=(mate, place), device_id_type=MESH,
        )

    def total_copy(g, k, q):
        return pltpu.make_async_remote_copy(
            src_ref=total.at[(g * per + k) * halves + q], dst_ref=recv.at[slot],
            send_sem=send3, recv_sem=recv3,
            device_id=(base + index(g, k), 2 * q + core), device_id_type=MESH,
        )

    def hand_out(g):
        mate_copy(g).wait_recv()
        for k in range(per):
            for q in range(halves):
                spot = (g * per + k) * halves + q
                total[spot] = (
                    acc[g, k, core, q] + mate_in[g, k, q].astype(jnp.float32)
                ).astype(total.dtype)
                here = jnp.logical_and(base + index(g, k) == me, 2 * q + core == place)

                @pl.when(here)
                def _():
                    pltpu.make_async_copy(total.at[spot], recv.at[slot], recv3).start()

                @pl.when(jnp.logical_not(here))
                def _():
                    total_copy(g, k, q).start()

    for sub in range(subs):
        own_copy(sub).wait()
        drain(gat[sub].at[pl.ds(0, N - 1)], recv1.at[sub])
        pivots(sub)
        if sub < subs - 1:
            def several(g, sub=sub):
                tiles(sub, g)

            loop(groups, several)
    for g in range(groups):
        tiles(subs - 1, g)
        for k in range(per):
            part[g, k] = acc[g, k, 1 - core].astype(part.dtype)
        mate_copy(g).start()
        if g > 0:
            hand_out(g - 1)
    hand_out(groups - 1)

    drain(norm_all.at[pl.ds(0, N - 1)], recvn)
    lane = lax.broadcasted_iota(jnp.int32, (1, LANES), 1)
    line = lax.broadcasted_iota(jnp.int32, (share, LANES), 0)
    cols = lax.broadcasted_iota(jnp.int32, (share, LANES), 1)
    own_norms = jnp.sum(
        jnp.where(cols == line + place * share, norm_src[0:1, :], 0.0), axis=1, keepdims=True
    )
    partner_norms = [norm_all[lax.rem(me + offsets[t], N)][0:1, 0:rows] for t in range(noff)]
    divisors = []
    for t in range(noff):
        for s in range(npiv):
            row = norm_all[pivot_block[t, s]][0:1, :]
            pivot_norm = jnp.sum(
                jnp.where(lane == pivot_row[t, s], row, 0.0), axis=1, keepdims=True
            )
            divisors.append((own_norms * pivot_norm) * partner_norms[t])

    slots = (G // 2) * NF

    for sub in range(subs):
        drain(gat[sub].at[pl.ds(0, N - 1)], send1.at[sub])
    drain(norm_all.at[pl.ds(0, N - 1)], sendn)
    for g in range(groups):
        mate_copy(g).wait_send()

    drain(recv, recv3)
    for s in range(npiv):
        whole = recv[0, s].astype(jnp.float32)
        for k in range(1, slots):
            whole = whole + recv[k, s].astype(jnp.float32)
        for t in range(noff):
            out[t, s] = (
                whole[:, t * rows : (t + 1) * rows] / divisors[t * npiv + s]
            ).astype(out.dtype)

    @pl.when(gathers)
    def _():
        drain(total.at[pl.ds(0, G * halves - 1)], send3)

    @pl.when(jnp.logical_not(gathers))
    def _():
        drain(total, send3)


def body(vectors, norms, offsets, pivot_block, pivot_row):
    rows, fields = vectors.shape
    N, NF = lax.axis_size("blk"), lax.axis_size("fld")
    noff, npiv = pivot_block.shape
    G = min(N, fields // LANES)
    C = fields // G
    widths = (C // 2, C // 2) if C % (2 * LANES) == 0 else (C,)
    groups = 4 if G % 4 == 0 else 1
    per = G // groups
    share = rows // NF
    halves = NF // 2
    wire = jnp.bfloat16 if share % 16 == 0 else jnp.float32
    wide = noff * rows
    slots = (G // 2) * NF
    subs = len(widths)
    dims = (N, NF, G, C, widths, groups, rows, noff, npiv)
    dma = pltpu.SemaphoreType.DMA
    anywhere = pl.BlockSpec(memory_space=pl.ANY)
    return pl.pallas_call(
        functools.partial(kernel, dims),
        out_shape=jax.ShapeDtypeStruct((noff, npiv, share, rows), jnp.bfloat16),
        in_specs=[anywhere] * 5,
        out_specs=pl.BlockSpec(memory_space=pltpu.VMEM),
        scratch_shapes=[
            pltpu.SMEM(offsets.shape, jnp.int32),
            pltpu.SMEM(pivot_block.shape, jnp.int32),
            pltpu.SMEM(pivot_row.shape, jnp.int32),
            pltpu.VMEM((1, rows), jnp.bfloat16),
            dma((4,)),
            tuple(pltpu.VMEM((N, rows, width), jnp.bfloat16) for width in widths),
            pltpu.VMEM((8, LANES), jnp.float32),
            pltpu.VMEM((N, 8, LANES), jnp.float32),
            pltpu.VMEM((noff * npiv, 16, max(widths)), jnp.bfloat16),
            pltpu.VMEM((groups, per, 2, halves, npiv, share, wide), jnp.float32),
            pltpu.VMEM((groups, per, halves, npiv, share, wide), wire),
            pltpu.VMEM((groups, per, halves, npiv, share, wide), wire),
            pltpu.VMEM((G * halves, npiv, share, wide), wire),
            pltpu.VMEM((slots, npiv, share, wide), wire),
            dma((subs,)),
            dma((subs,)),
            dma((subs,)),
            dma,
            dma,
            dma((groups,)),
            dma((groups,)),
            dma,
            dma,
        ],
        compiler_params=pltpu.CompilerParams(
            collective_id=0, has_side_effects=True, vmem_limit_bytes=63 * 1024 * 1024
        ),
        cost_estimate=pl.CostEstimate(
            flops=2 * noff * npiv * G * rows * rows * C,
            bytes_accessed=2 * rows * fields * 2,
            transcendentals=0,
        ),
    )(offsets, pivot_block, pivot_row, vectors, norms.reshape(1, rows))


def solution(mesh):
    return jax.shard_map(
        body,
        mesh=mesh,
        in_specs=(P("blk", "fld"), P("blk"), P(), P(), P()),
        out_specs=P(None, None, ("blk", "fld"), None),
        check_vma=False,
    )
```

```python
import functools

import jax
import jax.numpy as jnp
from jax import lax
from jax.experimental import pallas as pl
from jax.experimental.pallas import tpu as pltpu
from jax.sharding import PartitionSpec as P

MESH = pl.DeviceIdType.MESH
LANES = 128


def kernel(
    dims, offsets_in, pivot_block_in, pivot_row_in, vectors, norms_in, out,
    offsets, pivot_block, pivot_row, norms, small, gat, norm_src, norm_all, piv, acc, part, mate_in, total, recv,
    send1, recv1, own1, sendn, recvn, send2, recv2, send3, recv3,
):
    N, NF, G, C, widths, groups, rows, noff, npiv = dims
    share = rows // NF
    halves = NF // 2
    subs = len(widths)
    starts = [sum(widths[:sub]) for sub in range(subs)]
    per = G // groups
    me, place = lax.axis_index("blk"), lax.axis_index("fld")
    group, chunk = me // G, me % G
    base = group * G
    core = me % 2
    mate = me + 1 - 2 * core
    slot = (chunk // 2) * NF + place
    gathers = place % 2 == core

    barrier = pltpu.get_barrier_semaphore()

    for j in range(1, N):
        pl.semaphore_signal(
            barrier, inc=1, device_id=(lax.rem(me + j, N), place), device_id_type=MESH
        )
    for f in range(1, NF):
        for j in range(G):
            pl.semaphore_signal(
                barrier, inc=1, device_id=(base + j, lax.rem(place + f, NF)), device_id_type=MESH
            )

    smalls = [
        pltpu.make_async_copy(src, dst, small.at[k])
        for k, (src, dst) in enumerate((
            (norms_in, norms), (offsets_in, offsets),
            (pivot_block_in, pivot_block), (pivot_row_in, pivot_row),
        ))
    ]

    def own_copy(sub):
        first = pl.multiple_of(chunk * C + starts[sub], LANES)
        return pltpu.make_async_copy(
            vectors.at[:, pl.ds(first, widths[sub])], gat[sub].at[me], own1.at[sub]
        )

    for copy in smalls:
        copy.start()
    for sub in range(subs):
        own_copy(sub).start()
    norm_src[...] = jnp.zeros_like(norm_src)
    smalls[0].wait()
    norm_src[0:1, 0:rows] = norms[...].astype(jnp.float32)
    norm_all[me] = norm_src[...]
    pl.semaphore_wait(barrier, (N - 1) + G * (NF - 1))

    side = N // 2

    def peer_of(k):
        half, spot = me // side, me % side
        turn = lax.rem(spot + (k + 1) // 2, side)
        return (1 - half if k % 2 == 0 else half) * side + turn

    def block_copy(sub, k):
        peer = peer_of(k)
        first = pl.multiple_of((peer % G) * C + starts[sub], LANES)
        return pltpu.make_async_remote_copy(
            src_ref=vectors.at[:, pl.ds(first, widths[sub])], dst_ref=gat[sub].at[me],
            send_sem=send1.at[sub], recv_sem=recv1.at[sub],
            device_id=(peer, place), device_id_type=MESH,
        )

    def norm_copy(k):
        return pltpu.make_async_remote_copy(
            src_ref=norm_src, dst_ref=norm_all.at[me],
            send_sem=sendn, recv_sem=recvn,
            device_id=(peer_of(k), place), device_id_type=MESH,
        )

    def drain(ref, sem):
        pltpu.make_async_copy(ref, ref, sem).wait()

    def loop(count, step):
        def run(k, carry):
            step(k)
            return carry

        lax.fori_loop(0, count, run, 0)

    for sub in range(subs):
        for k in range(N - 1):
            block_copy(sub, k).start()
    for k in range(N - 1):
        norm_copy(k).start()

    for copy in smalls[1:]:
        copy.wait()

    def pivots(sub):
        width = widths[sub]
        spot = lax.broadcasted_iota(jnp.int32, (rows, width), 0)
        for t in range(noff):
            for s in range(npiv):
                block = gat[sub][pivot_block[t, s]].astype(jnp.float32)
                picked = jnp.sum(
                    jnp.where(spot == pivot_row[t, s], block, 0.0), axis=0, keepdims=True
                )
                piv[t * npiv + s, :, 0:width] = jnp.broadcast_to(picked, (16, width)).astype(jnp.bfloat16)

    def index(g, k):
        return k * groups + (g + (groups // 2) * (k % 2)) % groups

    def tile(sub, g, k):
        block, width = base + index(g, k), widths[sub]
        resident = gat[sub][block].reshape(rows // 16, 16, width)
        ahead = [block + offsets[t] for t in range(noff)]
        partner = jnp.concatenate(
            [gat[sub][jnp.where(b < N, b, b - N)] for b in ahead], axis=0
        )
        scaled = jnp.concatenate(
            [
                (resident * piv[j, :, 0:width][None]).reshape(rows, width)
                for j in range(noff * npiv)
            ],
            axis=0,
        )
        met = lax.dot_general(
            scaled, partner, (((1,), (1,)), ((), ())), preferred_element_type=jnp.float32
        )
        lane = lax.broadcasted_iota(jnp.int32, (npiv * rows, noff * rows), 1)
        value = met[0 : npiv * rows]
        for t in range(1, noff):
            value = jnp.where(
                lane < t * rows, value, met[t * npiv * rows : (t + 1) * npiv * rows]
            )
        pieces = {}
        for s in range(npiv):
            for h in range(NF):
                first = s * rows + h * share
                pieces[h % 2, h // 2, s] = value[first : first + share]
                if sub > 0:
                    pieces[h % 2, h // 2, s] += acc[g, k, h % 2, h // 2, s]
        return pieces

    def tiles(sub, g):
        for first in range(0, per, 2):
            pair = range(first, min(first + 2, per))
            found = [tile(sub, g, k) for k in pair]
            for k, pieces in zip(pair, found):
                for (c, q, s), piece in pieces.items():
                    acc[g, k, c, q, s] = piece

    def mate_copy(q):
        return pltpu.make_async_remote_copy(
            src_ref=part.at[q], dst_ref=mate_in.at[q],
            send_sem=send2.at[q], recv_sem=recv2.at[q],
            device_id=(mate, place), device_id_type=MESH,
        )

    def total_copy(g, k, q):
        return pltpu.make_async_remote_copy(
            src_ref=total.at[(g * per + k) * halves + q], dst_ref=recv.at[slot],
            send_sem=send3, recv_sem=recv3,
            device_id=(base + index(g, k), 2 * q + core), device_id_type=MESH,
        )

    def hand_out(g):
        mate_copy(g).wait_recv()
        for k in range(per):
            for q in range(halves):
                spot = (g * per + k) * halves + q
                total[spot] = (
                    acc[g, k, core, q] + mate_in[g, k, q].astype(jnp.float32)
                ).astype(total.dtype)
                here = jnp.logical_and(base + index(g, k) == me, 2 * q + core == place)

                @pl.when(here)
                def _():
                    pltpu.make_async_copy(total.at[spot], recv.at[slot], recv3).start()

                @pl.when(jnp.logical_not(here))
                def _():
                    total_copy(g, k, q).start()

    for sub in range(subs):
        own_copy(sub).wait()
        drain(gat[sub].at[pl.ds(0, N - 1)], recv1.at[sub])
        pivots(sub)
        if sub < subs - 1:
            def several(g, sub=sub):
                tiles(sub, g)

            loop(groups, several)
    for g in range(groups):
        tiles(subs - 1, g)
        for k in range(per):
            part[g, k] = acc[g, k, 1 - core].astype(part.dtype)
        mate_copy(g).start()
        if g > 0:
            hand_out(g - 1)
    hand_out(groups - 1)

    drain(norm_all.at[pl.ds(0, N - 1)], recvn)
    lane = lax.broadcasted_iota(jnp.int32, (1, LANES), 1)
    line = lax.broadcasted_iota(jnp.int32, (share, LANES), 0)
    cols = lax.broadcasted_iota(jnp.int32, (share, LANES), 1)
    own_norms = jnp.sum(
        jnp.where(cols == line + place * share, norm_src[0:1, :], 0.0), axis=1, keepdims=True
    )
    partner_norms = [norm_all[lax.rem(me + offsets[t], N)][0:1, 0:rows] for t in range(noff)]
    divisors = []
    for t in range(noff):
        for s in range(npiv):
            row = norm_all[pivot_block[t, s]][0:1, :]
            pivot_norm = jnp.sum(
                jnp.where(lane == pivot_row[t, s], row, 0.0), axis=1, keepdims=True
            )
            divisors.append((own_norms * pivot_norm) * partner_norms[t])

    slots = (G // 2) * NF

    for sub in range(subs):
        drain(gat[sub].at[pl.ds(0, N - 1)], send1.at[sub])
    drain(norm_all.at[pl.ds(0, N - 1)], sendn)
    for g in range(groups):
        mate_copy(g).wait_send()

    drain(recv, recv3)
    for s in range(npiv):
        whole = recv[0, s].astype(jnp.float32)
        for k in range(1, slots):
            whole = whole + recv[k, s].astype(jnp.float32)
        for t in range(noff):
            out[t, s] = (
                whole[:, t * rows : (t + 1) * rows] / divisors[t * npiv + s]
            ).astype(out.dtype)

    @pl.when(gathers)
    def _():
        drain(total.at[pl.ds(0, G * halves - 1)], send3)

    @pl.when(jnp.logical_not(gathers))
    def _():
        drain(total, send3)


def body(vectors, norms, offsets, pivot_block, pivot_row):
    rows, fields = vectors.shape
    N, NF = lax.axis_size("blk"), lax.axis_size("fld")
    noff, npiv = pivot_block.shape
    G = min(N, fields // LANES)
    C = fields // G
    widths = (C // 2, C // 2) if C % (2 * LANES) == 0 else (C,)
    groups = 4 if G % 4 == 0 else 1
    per = G // groups
    share = rows // NF
    halves = NF // 2
    wire = jnp.bfloat16 if share % 16 == 0 else jnp.float32
    wide = noff * rows
    slots = (G // 2) * NF
    subs = len(widths)
    dims = (N, NF, G, C, widths, groups, rows, noff, npiv)
    dma = pltpu.SemaphoreType.DMA
    anywhere = pl.BlockSpec(memory_space=pl.ANY)
    return pl.pallas_call(
        functools.partial(kernel, dims),
        out_shape=jax.ShapeDtypeStruct((noff, npiv, share, rows), jnp.bfloat16),
        in_specs=[anywhere] * 5,
        out_specs=pl.BlockSpec(memory_space=pltpu.VMEM),
        scratch_shapes=[
            pltpu.SMEM(offsets.shape, jnp.int32),
            pltpu.SMEM(pivot_block.shape, jnp.int32),
            pltpu.SMEM(pivot_row.shape, jnp.int32),
            pltpu.VMEM((1, rows), jnp.bfloat16),
            dma((4,)),
            tuple(pltpu.VMEM((N, rows, width), jnp.bfloat16) for width in widths),
            pltpu.VMEM((8, LANES), jnp.float32),
            pltpu.VMEM((N, 8, LANES), jnp.float32),
            pltpu.VMEM((noff * npiv, 16, max(widths)), jnp.bfloat16),
            pltpu.VMEM((groups, per, 2, halves, npiv, share, wide), jnp.float32),
            pltpu.VMEM((groups, per, halves, npiv, share, wide), wire),
            pltpu.VMEM((groups, per, halves, npiv, share, wide), wire),
            pltpu.VMEM((G * halves, npiv, share, wide), wire),
            pltpu.VMEM((slots, npiv, share, wide), wire),
            dma((subs,)),
            dma((subs,)),
            dma((subs,)),
            dma,
            dma,
            dma((groups,)),
            dma((groups,)),
            dma,
            dma,
        ],
        compiler_params=pltpu.CompilerParams(
            collective_id=0, has_side_effects=True, vmem_limit_bytes=63 * 1024 * 1024
        ),
        cost_estimate=pl.CostEstimate(
            flops=2 * noff * npiv * G * rows * rows * C,
            bytes_accessed=2 * rows * fields * 2,
            transcendentals=0,
        ),
    )(offsets, pivot_block, pivot_row, vectors, norms.reshape(1, rows))


def solution(mesh):
    return jax.shard_map(
        body,
        mesh=mesh,
        in_specs=(P("blk", "fld"), P("blk"), P(), P(), P()),
        out_specs=P(None, None, ("blk", "fld"), None),
        check_vma=False,
    )
```
